128 devices in a mesh: sp: 8 (over z, core), ep: 16 (over y, x).
Axes of the slice: x: 4, y: 4, z: 4, core: 2. Of those that a mesh axis runs over, the one named last changes fastest.
Arguments:
- hidden_in: bfloat16 [16, 1024, 6144], P('ep', 'sp'), may hold values from -6 to 6
- norm_gain: float32 [6144], replicated, may hold values from 0.25 to 4
- d_layer: bfloat16 [16, 1024, 6144], P('ep', 'sp'), may hold values from -6 to 6
- route_ids: int32 [16, 1024, 8], P('ep', 'sp'), may hold values from 0 to 159, as said below
- route_gates: float32 [16, 1024, 8], P('ep', 'sp'), may hold values from 0.1 to 1
- gate_weight: bfloat16 [16, 6144, 2560], P('ep', None, 'sp'), may hold values from -0.078125 to 0.078125
- up_weight: bfloat16 [16, 6144, 2560], P('ep', None, 'sp'), may hold values from -0.078125 to 0.078125
- down_weight: bfloat16 [16, 2560, 6144], P('ep', 'sp'), may hold values from -0.125 to 0.125
- saved_preact: bfloat16 [16, 2, 1024, 2560], P('ep', None, None, 'sp'), may hold values from -6 to 6
- queries: bfloat16 [16, 1024, 6144], P('ep', 'sp'), may hold values from -6 to 6
- key_vectors: bfloat16 [16, 1024, 512], P('ep', 'sp'), may hold values from -6 to 6
- value_vectors: bfloat16 [16, 1024, 512], P('ep', 'sp'), may hold values from -6 to 6
Outputs:
- moe_grad: bfloat16 [16, 1024, 6144], P('ep', 'sp')
- d_queries: bfloat16 [16, 1024, 6144], P('ep', 'sp')
- d_keys: bfloat16 [16, 1024, 512], P('ep', 'sp')
- d_values: bfloat16 [16, 1024, 512], P('ep', 'sp')
The draws below stay inside these ranges and needn't reach their ends.
Inputs may be any that keep to these rules, and one draw needn't show every extreme that they name: `route_ids`: each token names 8 different experts. Among the tokens of one block (one device's 128 tokens), no expert is named by more than 8 tokens, and in every block one of the experts below 16 is named by exactly 8.
All inputs are finite; a program needn't handle non-finite values.
Results may differ from the reference program's by a relative error of at most 0.017.
Values may be sent and summed in bfloat16 or wider, within the bound.
No kernel may reach another device: no remote copies, remote signals or barrier semaphores. Data moves between devices by JAX's collectives and lax.ppermute only.
A program may use at most 128 MiB of HBM per device.

```python
import math
import jax
import jax.numpy as jnp
from jax import lax

D = 6144
FF = 2560
HD = 128
NUM_EXPERTS = 160
TOPK = 8
HEADS = 48
KV = 4
TOK_DEV = 128
CAP = 8
SEQS = 16
LENGTH = 1024
EXPERTS = 16
FF_SHARD = 320
ROWS = 1024
N_SP = 8


def draw_route_ids(key, part):
    key = jax.random.fold_in(key, 11)
    blocks = SEQS * LENGTH // TOK_DEV
    key_one, key_two, key_three, key_four = jax.random.split(key, 4)
    hot_expert = jnp.minimum(jax.random.randint(key_one, (blocks,), 0, EXPERTS), jax.random.randint(key_two, (blocks,), 0, EXPERTS))
    orders = jax.vmap(lambda sub: jax.random.permutation(sub, NUM_EXPERTS))(jax.random.split(key_three, blocks))
    token_order = jax.vmap(lambda sub: jax.random.permutation(sub, TOK_DEV))(jax.random.split(key_four, blocks))
    hot_at = jnp.argmax((orders == hot_expert[:, None]).astype(jnp.int32), axis=1)
    index = jnp.arange(NUM_EXPERTS - 1)
    others = jnp.where(index[None, :] < hot_at[:, None], orders[:, index], orders[:, index + 1])
    choice_idx = jnp.arange(TOPK)[None, None, :]
    flat_index = (token_order[:, :, None] * TOPK + choice_idx) % (NUM_EXPERTS - 1)
    chosen = jax.vmap(lambda row, where_idx: row[where_idx])(others, flat_index)
    is_hot = (token_order[:, :, None] < CAP) & (choice_idx == token_order[:, :, None] % TOPK)
    routes = jnp.where(is_hot, hot_expert[:, None, None], chosen)
    return routes.reshape(SEQS, LENGTH, TOPK).astype(jnp.int32)


def draw_key_vectors(key, part):
    key = jax.random.fold_in(key, 21)
    values = jnp.clip(jax.random.normal(key, (SEQS, LENGTH, KV, HD), jnp.float32), -6.0, 6.0)
    return values.reshape(SEQS, LENGTH, KV * HD).astype(jnp.bfloat16)


def draw_queries(key, part):
    key = jax.random.fold_in(key, 22)
    values = jnp.clip(jax.random.normal(key, (SEQS, LENGTH, HEADS, HD), jnp.float32), -6.0, 6.0)
    return values.reshape(SEQS, LENGTH, HEADS * HD).astype(jnp.bfloat16)


def shard_levels(own_key, dims, cuts, low, largest):
    level, own = 1.0, jax.random.fold_in(own_key, 6)
    for dim, blocks in cuts:
        heights = jnp.exp(jax.random.uniform(jax.random.fold_in(own, dim), (blocks,), jnp.float32, low / len(cuts), largest / len(cuts)))
        level = level * jnp.repeat(heights, dims[dim] // blocks).reshape([-1 if axis == dim else 1 for axis in range(len(dims))])
    return level


def centred(stream_key, extent, scale, limit, shards=(), kind=jnp.bfloat16):
    level = shard_levels(stream_key, extent, shards, -0.22, 0.18) if shards else 1.0
    array = jax.random.normal(stream_key, extent, jnp.float32) * scale * level
    return jnp.minimum(jnp.maximum(array, -limit), limit).astype(kind)


def setup_inputs(seed: int = 0) -> dict:
    arg_keys = jax.random.split(jax.random.key(seed), 13)
    return {
        "hidden_in": centred(arg_keys[0], (SEQS, LENGTH, D), 1.0, 6.0, ((0, 16), (1, 8))),
        "norm_gain": jnp.clip(jnp.exp(jax.random.uniform(arg_keys[1], (D,), jnp.float32, math.log(0.25), math.log(4.0))), 0.25, 4.0),
        "d_layer": centred(arg_keys[2], (SEQS, LENGTH, D), 1.0, 6.0, ((0, 16), (1, 8))),
        "route_ids": draw_route_ids(jax.random.fold_in(arg_keys[12], 71), 0),
        "route_gates": jnp.clip(0.1 + 0.9 * jax.random.uniform(arg_keys[4], (SEQS, LENGTH, TOPK), jnp.float32) ** shard_levels(arg_keys[4], (SEQS, LENGTH, TOPK), ((0, 16), (1, 8)), -0.2, 0.2), 0.1, 1.0),
        "gate_weight": centred(arg_keys[5], (EXPERTS, D, FF), D ** -0.5, 0.078125, ((0, 16), (2, 8))),
        "up_weight": centred(arg_keys[6], (EXPERTS, D, FF), D ** -0.5, 0.078125, ((0, 16), (2, 8))),
        "down_weight": centred(arg_keys[7], (EXPERTS, FF, D), FF ** -0.5, 0.125, ((0, 16), (1, 8))),
        "saved_preact": centred(arg_keys[8], (EXPERTS, 2, ROWS, FF), 1.5, 6.0, ((0, 16), (3, 8))),
        "queries": draw_queries(jax.random.fold_in(arg_keys[12], 71), 0),
        "key_vectors": draw_key_vectors(jax.random.fold_in(arg_keys[12], 71), 0),
        "value_vectors": centred(arg_keys[11], (SEQS, LENGTH, KV * HD), 1.0, 6.0, ((0, 16), (1, 8))),
    }


def route_table(route_list, slots, experts):
    route_count = route_list.shape[0]
    onehot = (route_list[:, None] == jnp.arange(experts, dtype=jnp.int32)[None, :]).astype(jnp.int32)
    earlier = jnp.cumsum(onehot, axis=0) - onehot
    slot_pos = lax.optimization_barrier(jnp.sum(earlier * onehot, axis=1)).astype(jnp.int32)
    target = jnp.where(route_list < experts, route_list * slots + slot_pos, -1).astype(jnp.int32)
    matches = target[None, :] == jnp.arange(experts * slots, dtype=jnp.int32)[:, None]
    source = lax.optimization_barrier(jnp.sum(jnp.where(matches, jnp.arange(route_count, dtype=jnp.int32)[None, :], 0), axis=1)).astype(jnp.int32)
    filled = jnp.any(matches, axis=1)
    return (source, filled)

def dispatch_rows(grad_rows, gate_list, source, filled):
    picked = jnp.take(grad_rows, source // TOPK, axis=0).astype(jnp.float32) * gate_list[source][:, None]
    return jnp.where(filled[:, None], picked, 0.0).astype(jnp.bfloat16)

def collect_rows(returned, source, filled):
    token_of = source // TOPK
    token_match = ((token_of[None, :] == jnp.arange(TOK_DEV, dtype=jnp.int32)[:, None]) & filled[None, :]).astype(jnp.bfloat16)
    return jnp.dot(token_match, returned, preferred_element_type=jnp.float32)

def expert_back(picked, saved_gate, saved_up, gate_cols, up_cols, down_rows):
    d_act = jnp.dot(picked, down_rows.T, preferred_element_type=jnp.float32)
    gate_val = saved_gate.astype(jnp.float32)
    up_val = saved_up.astype(jnp.float32)
    sigmoid_g = jax.nn.sigmoid(gate_val)
    d_gate = (d_act * up_val * sigmoid_g * (1.0 + gate_val * (1.0 - sigmoid_g))).astype(jnp.bfloat16)
    d_up = (d_act * gate_val * sigmoid_g).astype(jnp.bfloat16)

    def add_shard(shard_idx, running):
        low = shard_idx * FF_SHARD
        gate_part = lax.dynamic_slice_in_dim(d_gate, low, FF_SHARD, 1)
        up_part = lax.dynamic_slice_in_dim(d_up, low, FF_SHARD, 1)
        gate_block = lax.dynamic_slice_in_dim(gate_cols, low, FF_SHARD, 1)
        up_block = lax.dynamic_slice_in_dim(up_cols, low, FF_SHARD, 1)
        term = jnp.dot(gate_part, gate_block.T, preferred_element_type=jnp.float32)
        term = term + jnp.dot(up_part, up_block.T, preferred_element_type=jnp.float32)
        rounded = lax.optimization_barrier(term.astype(jnp.bfloat16))
        return running + rounded.astype(jnp.float32)
    summed = lax.fori_loop(0, N_SP, add_shard, jnp.zeros((picked.shape[0], picked.shape[1]), jnp.float32))
    return summed.astype(jnp.bfloat16)

def attend_heads(query_heads, grad_heads, key_head, value_head):
    length = query_heads.shape[0]
    head_count = query_heads.shape[1]
    width = query_heads.shape[2]
    score_scale = 1.0 / math.sqrt(width)
    causal = jnp.arange(length)[None, :] <= jnp.arange(length)[:, None]

    def per_head(carry, head_idx):
        grad_key, grad_value = carry
        query_one = lax.dynamic_index_in_dim(query_heads, head_idx, 1, keepdims=False)
        grad_one = lax.dynamic_index_in_dim(grad_heads, head_idx, 1, keepdims=False)
        scores = jnp.dot(query_one, key_head.T, preferred_element_type=jnp.float32) * score_scale
        scores = jnp.where(causal, scores, -jnp.inf)
        top = lax.optimization_barrier(jnp.max(scores, axis=1, keepdims=True))
        expo = jnp.exp(scores - top)
        attn_prob = expo / lax.optimization_barrier(jnp.sum(expo, axis=1, keepdims=True))
        prob_rounded = attn_prob.astype(jnp.bfloat16)
        attn_out = jnp.dot(prob_rounded, value_head, preferred_element_type=jnp.float32)
        row_delta = lax.optimization_barrier(jnp.sum(grad_one.astype(jnp.float32) * attn_out, axis=1, keepdims=True))
        d_prob = jnp.dot(grad_one, value_head.T, preferred_element_type=jnp.float32)
        d_score = (attn_prob * (d_prob - row_delta) * score_scale).astype(jnp.bfloat16)
        grad_query = jnp.dot(d_score, key_head, preferred_element_type=jnp.float32).astype(jnp.bfloat16)
        grad_key = grad_key + jnp.dot(d_score.T, query_one, preferred_element_type=jnp.float32)
        grad_value = grad_value + jnp.dot(prob_rounded.T, grad_one, preferred_element_type=jnp.float32)
        return ((grad_key, grad_value), grad_query)
    start = (jnp.zeros((length, width), jnp.float32), jnp.zeros((length, width), jnp.float32))
    (grad_key, grad_value), grad_query = lax.scan(per_head, start, jnp.arange(head_count))
    return (grad_query, grad_key, grad_value)

def reference(hidden_in, norm_gain, d_layer, route_ids, route_gates, gate_weight, up_weight, down_weight, saved_preact, queries, key_vectors, value_vectors):
    blocks = SEQS * N_SP
    route_list = route_ids.reshape(blocks, TOK_DEV * TOPK)
    gate_list = route_gates.reshape(blocks, TOK_DEV * TOPK)
    grad_rows = d_layer.reshape(blocks, TOK_DEV, D)
    source, filled = jax.vmap(lambda ids_row: route_table(ids_row, CAP, EXPERTS))(route_list)
    sent = jax.vmap(dispatch_rows)(grad_rows, gate_list, source, filled)
    expert_in = sent.reshape(SEQS, N_SP, EXPERTS, CAP, D).transpose(2, 1, 0, 3, 4).reshape(EXPERTS, ROWS, D)

    def one_expert(expert_idx):
        return expert_back(expert_in[expert_idx], saved_preact[expert_idx, 0], saved_preact[expert_idx, 1], gate_weight[expert_idx], up_weight[expert_idx], down_weight[expert_idx])
    returned = lax.map(one_expert, jnp.arange(EXPERTS))
    returned = returned.reshape(EXPERTS, N_SP, SEQS, CAP, D).transpose(2, 1, 0, 3, 4).reshape(blocks, EXPERTS * CAP, D)
    d_normed = jax.vmap(collect_rows)(returned, source, filled).reshape(SEQS, LENGTH, D)
    stream = hidden_in.astype(jnp.float32)
    inverse = lax.rsqrt(lax.optimization_barrier(jnp.mean(stream * stream, axis=-1, keepdims=True)) + 1e-06)
    scaled = d_normed * norm_gain
    moe_value = inverse * scaled - stream * inverse ** 3 * lax.optimization_barrier(jnp.mean(stream * scaled, axis=-1, keepdims=True))
    moe_grad = moe_value.astype(jnp.bfloat16)
    d_attn = (d_layer.astype(jnp.float32) + moe_value).astype(jnp.bfloat16)
    group_size = HEADS // KV
    query_all = queries.reshape(SEQS, LENGTH, KV, group_size, HD)
    grad_all = d_attn.reshape(SEQS, LENGTH, KV, group_size, HD)
    key_all = key_vectors.reshape(SEQS, LENGTH, KV, HD)
    value_all = value_vectors.reshape(SEQS, LENGTH, KV, HD)

    def one_group(flat_idx):
        seq_idx = flat_idx // KV
        kv_idx = flat_idx % KV
        return attend_heads(query_all[seq_idx, :, kv_idx], grad_all[seq_idx, :, kv_idx], key_all[seq_idx, :, kv_idx], value_all[seq_idx, :, kv_idx])
    grad_query, grad_key, grad_value = lax.map(one_group, jnp.arange(SEQS * KV))
    d_queries = grad_query.reshape(SEQS, KV, group_size, LENGTH, HD).transpose(0, 3, 1, 2, 4).reshape(SEQS, LENGTH, D)
    d_keys = grad_key.astype(jnp.bfloat16).reshape(SEQS, KV, LENGTH, HD).transpose(0, 2, 1, 3).reshape(SEQS, LENGTH, KV * HD)
    d_values = grad_value.astype(jnp.bfloat16).reshape(SEQS, KV, LENGTH, HD).transpose(0, 2, 1, 3).reshape(SEQS, LENGTH, KV * HD)
    return (moe_grad, d_queries, d_keys, d_values)
```

```python
import math

import jax
import jax.numpy as jnp
from jax import lax
from jax.experimental import pallas as pl
from jax.experimental.pallas import tpu as pltpu
from jax.sharding import Mesh, PartitionSpec as P

D = 6144
HALF = 3072
FS = 320
HD = 128
TOK = 128
TOPK = 8
CAP = 8
HEADS = 48
KV = 4
EXPERTS = 16
LENGTH = 1024
BLOCK = 256
PAIRS = HEADS // 2
TILE = 512
OUT_CHUNKS = ((0, 1536), (1536, 1536))
BACK_CHUNKS = ((0, 1536), (1536, 1536))
F32 = jnp.float32
BF16 = jnp.bfloat16
MIB = 1024 * 1024

NT = (((1,), (1,)), ((), ()))


def params(mib):
    return pltpu.CompilerParams(vmem_limit_bytes=mib * MIB)


def dot(a, b):
    return jnp.dot(a, b, preferred_element_type=F32)


def dot_nt(a, b):
    return lax.dot_general(a, b, NT, preferred_element_type=F32)


def dispatch_kernel(ids_ref, gates_ref, rows_ref, collect_ref, *sent_refs):
    ids = ids_ref[...]
    gates = gates_ref[...]
    row = lax.broadcasted_iota(jnp.int32, (TOK, TOK), 0)
    col = lax.broadcasted_iota(jnp.int32, (TOK, TOK), 1)
    hit_t = jnp.zeros((TOK, TOK), F32)
    gate_t = jnp.zeros((TOK, TOK), F32)
    for k in range(TOPK):
        match = ids[:, k : k + 1] == col
        hit_t = hit_t + jnp.where(match, 1.0, 0.0)
        gate_t = gate_t + jnp.where(match, gates[:, k : k + 1], 0.0)
    earlier = jnp.where(row > col, 1.0, 0.0).astype(BF16)
    slot_t = dot(earlier, hit_t.astype(BF16))
    hit = hit_t.T[:EXPERTS]
    slot = slot_t.T[:EXPERTS]
    gate = gate_t.T[:EXPERTS]
    want = lax.broadcasted_iota(jnp.int32, (EXPERTS, CAP, TOK), 1).astype(F32)
    pick3 = jnp.where((hit[:, None, :] > 0.5) & (slot[:, None, :] == want), 1.0, 0.0)
    gate3 = jnp.sum(pick3 * gate[:, None, :], axis=2, keepdims=True)
    pick = pick3.reshape(EXPERTS * CAP, TOK)
    gate_col = gate3.reshape(EXPERTS * CAP, 1)
    collect_ref[...] = pick.T.astype(BF16)
    pick = pick.astype(BF16)
    for (low, width), sent_ref in zip(OUT_CHUNKS, sent_refs):
        for half in range(2):
            start = half * HALF + low
            rows = rows_ref[:, start : start + width]
            sent_ref[half * TOK : (half + 1) * TOK, :] = (dot(pick, rows) * gate_col).astype(BF16)


def dispatch(ids, gates, rows):
    outs = [jax.ShapeDtypeStruct((TOK, EXPERTS * CAP), BF16)]
    outs += [jax.ShapeDtypeStruct((BLOCK, width), BF16) for _, width in OUT_CHUNKS]
    return pl.pallas_call(dispatch_kernel, out_shape=outs, compiler_params=params(40))(
        ids, gates, rows
    )


def act_kernel(count, first, last, where_ref, *refs):
    parts = refs[:count]
    own_ref, oth_ref = refs[count : count + 2]
    rest = refs[count + 2 :]
    if not first:
        before_ref, rest = rest[0], rest[1:]
    total_ref = rest[0]
    step = pl.program_id(0)

    @pl.when(step == 0)
    def _():
        if first:
            total_ref[...] = jnp.zeros_like(total_ref)
        else:
            total_ref[...] = before_ref[...]

    for k in range(count):
        block = parts[k][...]
        total_ref[k, 0] += dot_nt(block, own_ref[...])
        total_ref[k, 1] += dot_nt(block, oth_ref[...])
    if last:

        @pl.when(step == pl.num_programs(0) - 1)
        def _():
            rest[1][...] = total_ref[...].astype(BF16)


def act(where, parts, before, last, low, down_own, down_oth):
    count = len(parts)
    width = parts[0].shape[1]
    base = low // TILE
    per_half = HALF // TILE
    whole = pl.BlockSpec((count, 2, BLOCK, FS), lambda i, w: (0, 0, 0, 0))
    in_specs = [pl.BlockSpec((BLOCK, TILE), lambda i, w: (0, i)) for _ in parts]
    in_specs.append(pl.BlockSpec((FS, TILE), lambda i, w: (0, w[0] * per_half + base + i)))
    in_specs.append(pl.BlockSpec((FS, TILE), lambda i, w: (0, base + i)))
    args = list(parts) + [down_own, down_oth]
    if before is not None:
        in_specs.append(whole)
        args.append(before)
    shape = (count, 2, BLOCK, FS)
    out_shape = [jax.ShapeDtypeStruct(shape, F32)]
    if last:
        out_shape.append(jax.ShapeDtypeStruct(shape, BF16))

    def kernel(*refs):
        act_kernel(count, before is None, last, *refs)

    return pl.pallas_call(
        kernel,
        grid_spec=pltpu.PrefetchScalarGridSpec(
            num_scalar_prefetch=1,
            grid=(width // TILE,),
            in_specs=in_specs,
            out_specs=[whole] * len(out_shape),
        ),
        out_shape=out_shape,
        compiler_params=params(40),
        cost_estimate=pl.CostEstimate(
            flops=2 * count * BLOCK * width * 2 * FS,
            bytes_accessed=2 * (count * BLOCK * width + 2 * FS * width) + 8 * count * BLOCK * FS,
            transcendentals=0,
        ),
    )(where, *args)


def back_kernel(where_ref, mine_ref, came_ref, saved_ref, saved_oth_ref, *refs):
    weights, (out_ref, pre_ref) = refs[:4], refs[4:]

    @pl.when(pl.program_id(0) == 0)
    def _():
        for part, saved in ((0, saved_ref), (1, saved_oth_ref)):
            d_act = mine_ref[0, part] + came_ref[0, 1 - part].astype(F32)
            gate = saved[0].astype(F32)
            up = saved[1].astype(F32)
            sg = 1.0 / (1.0 + jnp.exp(-gate))
            scaled = d_act * sg
            pre_ref[2 * part] = (scaled * up * (1.0 + gate * (1.0 - sg))).astype(BF16)
            pre_ref[2 * part + 1] = (scaled * gate).astype(BF16)

    total = dot_nt(pre_ref[0], weights[0][...])
    for k in range(1, 4):
        total = total + dot_nt(pre_ref[k], weights[k][...])
    out_ref[...] = total.astype(BF16)


def back(where, block, mine, mine_at, came, came_at, saved, saved_oth, weights, low, width):
    base = low // TILE
    per_half = HALF // TILE
    own = pl.BlockSpec((TILE, FS), lambda i, w: (w[0] * per_half + base + i, 0))
    oth = pl.BlockSpec((TILE, FS), lambda i, w: (base + i, 0))
    rows = pl.BlockSpec((2, BLOCK, FS), lambda i, w: (0, w[1 + block], 0))
    return pl.pallas_call(
        back_kernel,
        grid_spec=pltpu.PrefetchScalarGridSpec(
            num_scalar_prefetch=1,
            grid=(width // TILE,),
            in_specs=[
                pl.BlockSpec((1, 2, BLOCK, FS), lambda i, w: (mine_at, 0, 0, 0)),
                pl.BlockSpec((1, 2, BLOCK, FS), lambda i, w: (came_at, 0, 0, 0)),
                rows,
                rows,
                own,
                own,
                oth,
                oth,
            ],
            out_specs=pl.BlockSpec((BLOCK, TILE), lambda i, w: (0, i)),
            scratch_shapes=[pltpu.VMEM((4, BLOCK, FS), BF16)],
        ),
        out_shape=jax.ShapeDtypeStruct((BLOCK, width), BF16),
        compiler_params=params(40),
        cost_estimate=pl.CostEstimate(
            flops=2 * BLOCK * width * 4 * FS,
            bytes_accessed=2 * (4 * FS * width + BLOCK * width) + 12 * BLOCK * FS,
            transcendentals=2 * BLOCK * FS,
        ),
    )(where, mine, came, saved, saved_oth, *weights)


def combine_kernel(collect_ref, hidden_ref, layer_ref, gain_ref, *refs):
    returned = refs[: len(BACK_CHUNKS)]
    moe_ref, attn_ref, scaled_ref = refs[len(BACK_CHUNKS) :]
    collect = collect_ref[...]
    square = jnp.zeros((TOK, 1), F32)
    cross = jnp.zeros((TOK, 1), F32)
    for (low, width), ref in zip(BACK_CHUNKS, returned):
        for half in range(2):
            start = half * HALF + low
            normed = dot(collect, ref[half * TOK : (half + 1) * TOK, :])
            scaled = normed * gain_ref[:, start : start + width]
            stream = hidden_ref[:, start : start + width].astype(F32)
            scaled_ref[:, start : start + width] = scaled
            square = square + jnp.sum(stream * stream, axis=1, keepdims=True)
            cross = cross + jnp.sum(stream * scaled, axis=1, keepdims=True)
    inverse = lax.rsqrt(square / D + 1e-06)
    factor = inverse * inverse * inverse * (cross / D)
    for start in range(0, D, 768):
        cols = slice(start, start + 768)
        moe = inverse * scaled_ref[:, cols] - hidden_ref[:, cols].astype(F32) * factor
        moe_ref[:, cols] = moe.astype(BF16)
        attn_ref[:, cols] = (layer_ref[:, cols].astype(F32) + moe).astype(BF16)


def combine(collect, hidden, layer, gain, returned):
    return pl.pallas_call(
        combine_kernel,
        out_shape=[jax.ShapeDtypeStruct((TOK, D), BF16)] * 2,
        scratch_shapes=[pltpu.VMEM((TOK, D), F32)],
        compiler_params=params(40),
    )(collect, hidden, layer, gain, *returned)


def stack_pair(block):
    return jnp.concatenate([block[:, :HD], block[:, HD:]], axis=0)


def prob_kernel(where_ref, query_ref, key_ref, prob_ref):
    query = stack_pair(query_ref[...])
    scores = dot_nt(key_ref[...], query) * (1.0 / math.sqrt(HD))
    key_at = lax.broadcasted_iota(jnp.int32, (LENGTH, 2 * HD), 0)
    query_at = lax.broadcasted_iota(jnp.int32, (LENGTH, 2 * HD), 1) % HD + where_ref[5] * TOK
    scores = jnp.where(key_at <= query_at, scores, -jnp.inf)
    expo = jnp.exp(scores - jnp.max(scores, axis=0, keepdims=True))
    prob_ref[0] = (expo * (1.0 / jnp.sum(expo, axis=0, keepdims=True))).astype(BF16)


def probs(where, queries, kv):
    per_group = PAIRS // KV
    return pl.pallas_call(
        prob_kernel,
        grid_spec=pltpu.PrefetchScalarGridSpec(
            num_scalar_prefetch=1,
            grid=(PAIRS,),
            in_specs=[
                pl.BlockSpec((TOK, 2 * HD), lambda p, w: (0, p)),
                pl.BlockSpec((LENGTH, HD), lambda p, w: (0, p // per_group)),
            ],
            out_specs=pl.BlockSpec((1, LENGTH, 2 * HD), lambda p, w: (p, 0, 0)),
        ),
        out_shape=jax.ShapeDtypeStruct((PAIRS, LENGTH, 2 * HD), BF16),
        compiler_params=params(40),
        cost_estimate=pl.CostEstimate(
            flops=2 * HEADS * TOK * LENGTH * HD * 3,
            bytes_accessed=2 * HEADS * TOK * LENGTH,
            transcendentals=HEADS * TOK * LENGTH,
        ),
    )(where, queries, kv)


def attend_kernel(
    where_ref,
    prob_ref,
    query_ref,
    grad_ref,
    key_t_ref,
    value_ref,
    dq_ref,
    mine_ref,
    oth_ref,
    dk_ref,
    dv_ref,
):
    step = pl.program_id(1)
    prob = prob_ref[0]
    query = stack_pair(query_ref[...])
    grad = stack_pair(grad_ref[...])
    d_prob = dot_nt(value_ref[...], grad)
    wide = prob.astype(F32)
    delta = jnp.sum(wide * d_prob, axis=0, keepdims=True)
    d_score = (wide * (d_prob - delta) * (1.0 / math.sqrt(HD))).astype(BF16)
    dq_t = dot(key_t_ref[...], d_score)
    dq_ref[:, :HD] = dq_t[:, :HD].T.astype(BF16)
    dq_ref[:, HD:] = dq_t[:, HD:].T.astype(BF16)

    @pl.when(step == 0)
    def _():
        dk_ref[...] = jnp.zeros_like(dk_ref)
        dv_ref[...] = jnp.zeros_like(dv_ref)

    dk_ref[...] += dot(d_score, query)
    dv_ref[...] += dot(prob, grad)

    @pl.when(step == pl.num_programs(1) - 1)
    def _():
        core = where_ref[0]
        for k, out_k in ((0, 0), (1, 2), (2, 1), (3, 3)):
            z_k = where_ref[1 + k]
            at = pl.multiple_of((2 * z_k + core) * TOK, TOK)
            mine_ref[0, k] = dk_ref[pl.ds(at, TOK), :].astype(BF16)
            mine_ref[1, k] = dv_ref[pl.ds(at, TOK), :].astype(BF16)
            at = pl.multiple_of((2 * z_k + 1 - core) * TOK, TOK)
            oth_ref[0, out_k] = dk_ref[pl.ds(at, TOK), :].astype(BF16)
            oth_ref[1, out_k] = dv_ref[pl.ds(at, TOK), :].astype(BF16)


def attend(where, prob, queries, grads, key_t, kv):
    per_group = PAIRS // KV
    pair = pl.BlockSpec((TOK, 2 * HD), lambda g, p, w: (0, g * per_group + p))
    sums = pl.BlockSpec((2, 4, TOK, HD), lambda g, p, w: (0, 0, 0, g))
    sums_shape = jax.ShapeDtypeStruct((2, 4, TOK, KV * HD), BF16)
    return pl.pallas_call(
        attend_kernel,
        grid_spec=pltpu.PrefetchScalarGridSpec(
            num_scalar_prefetch=1,
            grid=(KV, per_group),
            in_specs=[
                pl.BlockSpec((1, LENGTH, 2 * HD), lambda g, p, w: (g * per_group + p, 0, 0)),
                pair,
                pair,
                pl.BlockSpec((HD, LENGTH), lambda g, p, w: (g, 0)),
                pl.BlockSpec((LENGTH, HD), lambda g, p, w: (0, KV + g)),
            ],
            out_specs=[pair, sums, sums],
            scratch_shapes=[pltpu.VMEM((LENGTH, HD), F32), pltpu.VMEM((LENGTH, HD), F32)],
        ),
        out_shape=[jax.ShapeDtypeStruct((TOK, D), BF16), sums_shape, sums_shape],
        compiler_params=params(40),
    )(where, prob, queries, grads, key_t, kv)


def add(*terms):
    total = terms[0].astype(F32)
    for term in terms[1:]:
        total = total + term.astype(F32)
    return total.astype(BF16)


def local(
    hidden_in,
    norm_gain,
    d_layer,
    route_ids,
    route_gates,
    gate_weight,
    up_weight,
    down_weight,
    saved_preact,
    queries,
    key_vectors,
    value_vectors,
):
    pos = lambda z, c: (z % 4) * 2 + c
    ring = [(z, c) for z in range(4) for c in range(2)]
    perm_a = [(pos(z, c), pos(z + 1 - 2 * c, c)) for z, c in ring]
    perm_b = [(pos(z, c), pos(z - 1 + 2 * c, c)) for z, c in ring]
    perm_core = [(pos(z, c), pos(z, 1 - c)) for z, c in ring]
    ring_axes = ("z", "core")
    send_a = lambda x: lax.ppermute(x, ring_axes, perm_a)
    send_b = lambda x: lax.ppermute(x, ring_axes, perm_b)
    send_core = lambda x: lax.ppermute(x, ring_axes, perm_core)

    def spread(x):
        split = x.reshape(2 * EXPERTS, CAP, x.shape[1])
        return lax.all_to_all(split, ("core", "ep"), 0, 0, tiled=True).reshape(x.shape)

    core = lax.axis_index("core")
    z = lax.axis_index("z")
    toward = 1 - 2 * core
    where = jnp.stack(
        [core, z, (z - toward) % 4, (z + toward) % 4, (z + 2) % 4, 2 * z + core]
    ).astype(jnp.int32)

    layer = d_layer[0]
    saved = saved_preact[0]
    gate_w, up_w, down_w = gate_weight[0], up_weight[0], down_weight[0]

    kv = jnp.concatenate([key_vectors[0], value_vectors[0]], axis=1)
    kv = lax.all_gather(kv, ring_axes, axis=0, tiled=True)

    sent = dispatch(route_ids[0], route_gates[0], layer)
    collect, sent = sent[0], sent[1:]
    held = [spread(x) for x in sent]

    away = (1 - core) * HALF
    down_oth = send_core(lax.dynamic_slice_in_dim(down_w, away, HALF, 1))
    gate_oth = send_core(lax.dynamic_slice_in_dim(gate_w, away, HALF, 0))
    up_oth = send_core(lax.dynamic_slice_in_dim(up_w, away, HALF, 0))
    saved_oth = send_core(saved)

    ring_a = [send_a(x) for x in held]
    ring_b = [send_b(x) for x in held]
    ring_c = [send_a(x) for x in ring_a]

    def act_all(groups):
        total = None
        count = len(OUT_CHUNKS)
        for i, (low, _) in enumerate(OUT_CHUNKS):
            last = i == count - 1
            result = act(where, [g[i] for g in groups], total, last, low, down_w, down_oth)
            total = result[0]
        return total, result[1]

    near, near_send = act_all([ring_a, ring_b])
    home, home_send = act_all([held])
    far, far_send = act_all([ring_c])
    near_came = send_core(near_send)
    home_came = send_core(home_send)
    far_came = send_core(far_send)

    weights = (gate_w, up_w, gate_oth, up_oth)

    def back_block(block, mine, mine_at, came, came_at, low, width):
        return back(
            where, block, mine, mine_at, came, came_at, saved, saved_oth, weights, low, width
        )

    returned = []
    for low, width in BACK_CHUNKS:
        direct = back_block(2, near, 1, near_came, 0, low, width)
        distant = back_block(3, far, 0, far_came, 0, low, width)
        merged = back_block(1, near, 0, near_came, 1, low, width)
        own = back_block(0, home, 0, home_came, 0, low, width)
        direct = send_a(direct)
        distant = send_b(distant)
        merged = send_b(add(merged, distant))
        returned.append(spread(add(own, direct, merged)))

    moe, d_attn = combine(collect, hidden_in[0], layer, norm_gain[None, :], returned)

    prob = probs(where, queries[0], kv)
    key_t = kv[:, : KV * HD].T
    d_query, mine, oth = attend(where, prob, queries[0], d_attn, key_t, kv)

    total = add(mine, send_core(oth))
    direct = send_a(total[:, 2])
    distant = send_b(total[:, 3])
    merged = send_b(add(total[:, 1], distant))
    d_kv = add(total[:, 0], direct, merged)
    return (moe[None], d_query[None], d_kv[0][None], d_kv[1][None])


def solution(mesh):
    split = Mesh(mesh.devices.reshape(4, 2, 16), ("z", "core", "ep"))
    sp = ("z", "core")
    rows = P("ep", sp, None)
    in_specs = (
        rows,
        P(),
        rows,
        rows,
        rows,
        P("ep", None, sp),
        P("ep", None, sp),
        rows,
        P("ep", None, None, sp),
        rows,
        rows,
        rows,
    )
    return jax.shard_map(
        local, mesh=split, in_specs=in_specs, out_specs=(rows,) * 4, check_vma=False
    )
```

```python
import math

import jax
import jax.numpy as jnp
from jax import lax
from jax.experimental import pallas as pl
from jax.experimental.pallas import tpu as pltpu
from jax.sharding import Mesh, PartitionSpec as P

D = 6144
HALF = 3072
FS = 320
HD = 128
TOK = 128
TOPK = 8
CAP = 8
HEADS = 48
KV = 4
EXPERTS = 16
LENGTH = 1024
BLOCK = 256
GROUP = HEADS // KV
TILE = 768
FACTOR_COST = 1
ACT_MIB = 24
LEAD_MIB = 24
PER_HALF = HALF // TILE
HEADS_STEP = 6
WIDE = HEADS_STEP * HD
STEPS = HEADS // HEADS_STEP
STEPS_GROUP = GROUP // HEADS_STEP
OUT_CHUNKS = ((0, 3072),)
BACK_CHUNKS = ((0, 3072),)
SCALE = 1.0 / math.sqrt(HD)
F32 = jnp.float32
BF16 = jnp.bfloat16

NT = (((1,), (1,)), ((), ()))


def params(mib=24):
    return pltpu.CompilerParams(vmem_limit_bytes=mib * 1024 * 1024)


def dot(a, b):
    return jnp.dot(a, b, preferred_element_type=F32)


def dot_nt(a, b):
    return lax.dot_general(a, b, NT, preferred_element_type=F32)


def cost(flops, moved, exps=0):
    return pl.CostEstimate(flops=flops, bytes_accessed=moved, transcendentals=exps)


def dispatch(ids, gates, rows, key, value, chunk):
    low, width = chunk

    def kernel(ids_ref, gates_ref, rows_ref, key_ref, value_ref, sent_ref, collect_ref, kv_ref):
        kv_ref[:, : KV * HD] = key_ref[...]
        kv_ref[:, KV * HD :] = value_ref[...]
        ids = ids_ref[...]
        gates = gates_ref[...]
        row = lax.broadcasted_iota(jnp.int32, (TOK, TOK), 0)
        col = lax.broadcasted_iota(jnp.int32, (TOK, TOK), 1)
        expert = lax.broadcasted_iota(jnp.int32, (EXPERTS, TOK), 0)
        hit = jnp.zeros((EXPERTS, TOK), F32)
        gate = jnp.zeros((EXPERTS, TOK), F32)
        for k in range(TOPK):
            match = ids[k : k + 1, :] == expert
            hit = hit + jnp.where(match, 1.0, 0.0)
            gate = gate + jnp.where(match, gates[k : k + 1, :], 0.0)
        earlier = jnp.where(row < col, 1.0, 0.0).astype(BF16)
        slot = dot(hit.astype(BF16), earlier)
        want = lax.broadcasted_iota(jnp.int32, (EXPERTS, CAP, TOK), 1).astype(F32)
        pick3 = jnp.where((hit[:, None, :] > 0.5) & (slot[:, None, :] == want), 1.0, 0.0)
        gate3 = jnp.sum(pick3 * gate[:, None, :], axis=2, keepdims=True)
        pick = pick3.reshape(EXPERTS * CAP, TOK)
        gate_col = gate3.reshape(EXPERTS * CAP, 1)
        collect_ref[...] = pick.T.astype(BF16)
        pick = pick.astype(BF16)
        for half in range(2):
            start = half * HALF + low
            picked = dot(pick, rows_ref[:, start : start + width]) * gate_col
            sent_ref[half * TOK : (half + 1) * TOK, :] = picked.astype(BF16)

    whole = lambda x: pl.BlockSpec(x.shape, lambda i: (0,) * x.ndim)
    args = (ids, gates, rows, key, value)
    out_shape = [
        jax.ShapeDtypeStruct((BLOCK, width), BF16),
        jax.ShapeDtypeStruct((TOK, EXPERTS * CAP), BF16),
        jax.ShapeDtypeStruct((TOK, 2 * KV * HD), BF16),
    ]
    return pl.pallas_call(
        kernel,
        grid=(1,),
        in_specs=[whole(x) for x in args],
        out_specs=[whole(x) for x in out_shape],
        out_shape=out_shape,
        name="dispatch",
        compiler_params=params(60),
    )(*args)


def in_chip_order(where_ref, own, oth, axis=0):
    even = where_ref[0] == 0
    return jnp.concatenate([jnp.where(even, own, oth), jnp.where(even, oth, own)], axis=axis)


def factor_kernel(where_ref, saved_ref, saved_oth_ref, out_ref):
    pieces = []
    for ref in (saved_ref, saved_oth_ref):
        gate = ref[0].astype(F32)
        sg = 1.0 / (1.0 + jnp.exp(-gate))
        pieces.append((ref[1].astype(F32) * sg * (1.0 + gate * (1.0 - sg)), gate * sg))
    for k in range(2):
        both = in_chip_order(where_ref, pieces[0][k], pieces[1][k])
        out_ref[:, k * 2 * FS : (k + 1) * 2 * FS] = both.T.astype(BF16)


def factors(where, saved, saved_oth):
    rows = pl.BlockSpec((2, FS, BLOCK), lambda i, w: (0, 0, i))
    return pl.pallas_call(
        factor_kernel,
        grid_spec=pltpu.PrefetchScalarGridSpec(
            num_scalar_prefetch=1,
            grid=(LENGTH // BLOCK,),
            in_specs=[rows, rows],
            out_specs=pl.BlockSpec((BLOCK, 4 * FS), lambda i, w: (i, 0)),
        ),
        out_shape=jax.ShapeDtypeStruct((LENGTH, 4 * FS), BF16),
        name="factors",
        compiler_params=params(16),
        cost_estimate=cost(FACTOR_COST * LENGTH * FS, FACTOR_COST * LENGTH * FS),
    )(where, saved, saved_oth)


def act(where, blocks, down_own, down_oth, mib, gates=()):
    count = len(blocks)
    shape = (count * BLOCK, 2 * FS)

    def kernel(where_ref, *refs):
        part_refs = refs[: count * len(OUT_CHUNKS)]
        own_ref, oth_ref = refs[count * len(OUT_CHUNKS) :][:2]
        total_ref, send_ref = refs[-2:]
        step = pl.program_id(0)
        weight = in_chip_order(where_ref, own_ref[...], oth_ref[...])

        @pl.when(step == 0)
        def _():
            total_ref[...] = jnp.zeros_like(total_ref)

        for c, (low, width) in enumerate(OUT_CHUNKS):
            start = low // TILE

            @pl.when((step >= start) & (step < start + width // TILE))
            def _():
                refs_c = part_refs[c * count : (c + 1) * count]
                rows = jnp.concatenate([ref[...] for ref in refs_c], axis=0)
                total_ref[...] += dot_nt(rows, weight)

        @pl.when(step == pl.num_programs(0) - 1)
        def _():
            send_ref[...] = total_ref[...].astype(BF16)

    whole = pl.BlockSpec(shape, lambda i, w: (0, 0))
    half = pl.BlockSpec((FS, TILE), lambda i, w: (0, w[0] * PER_HALF + i))
    parts = [block[c] for c in range(len(OUT_CHUNKS)) for block in blocks]
    return pl.pallas_call(
        kernel,
        grid_spec=pltpu.PrefetchScalarGridSpec(
            num_scalar_prefetch=1,
            grid=(PER_HALF,),
            in_specs=[chunk_spec(*c) for c in OUT_CHUNKS for _ in blocks]
            + [half, half]
            + [pl.BlockSpec(memory_space=pl.ANY)] * len(gates),
            out_specs=[whole, whole],
        ),
        out_shape=[jax.ShapeDtypeStruct(shape, F32), jax.ShapeDtypeStruct(shape, BF16)],
        name="act",
        compiler_params=params(mib),
        cost_estimate=cost(
            3 * 2 * count * BLOCK * HALF * 2 * FS,
            3 * 2 * (count * BLOCK * HALF + 2 * FS * HALF) + 3 * 6 * count * BLOCK * 2 * FS,
        ),
    )(where, *parts, down_own, down_oth, *gates)


def chunk_spec(low, width):
    start, steps = low // TILE, width // TILE
    return pl.BlockSpec((BLOCK, TILE), lambda i, w: (0, jnp.clip(i - start, 0, steps - 1)))


def back(where, blocks, factor, weights, mib, gates=()):
    count = len(blocks)

    def kernel(where_ref, *refs):
        act_refs, refs = refs[: 3 * count], refs[3 * count :]
        gate_own, up_own, gate_oth, up_oth = refs[:4]
        out_refs, pre_ref = refs[4 + len(gates) : -1], refs[-1]
        step = pl.program_id(0)

        @pl.when(step == 0)
        def _():
            for k in range(count):
                mine_ref, came_ref, factor_ref = act_refs[3 * k : 3 * k + 3]
                d_act = mine_ref[...] + came_ref[...].astype(F32)
                for side in range(2):
                    cols = slice(side * 2 * FS, (side + 1) * 2 * FS)
                    scaled = d_act * factor_ref[:, cols].astype(F32)
                    pre_ref[k * BLOCK : (k + 1) * BLOCK, cols] = scaled.astype(BF16)

        gate = in_chip_order(where_ref, gate_own[...], gate_oth[...])
        up = in_chip_order(where_ref, up_own[...], up_oth[...])
        weight = jnp.concatenate([gate, up], axis=0)
        total = dot(pre_ref[...], weight).astype(BF16)
        for c, (low, width) in enumerate(BACK_CHUNKS):
            start = low // TILE

            @pl.when((step >= start) & (step < start + width // TILE))
            def _():
                for k in range(count):
                    out_refs[c * count + k][...] = total[k * BLOCK : (k + 1) * BLOCK]

    def act_specs(block, _mine, at, _came, came_at):
        return [
            pl.BlockSpec((BLOCK, 2 * FS), lambda i, w: (at, 0)),
            pl.BlockSpec((BLOCK, 2 * FS), lambda i, w: (came_at, 0)),
            pl.BlockSpec((BLOCK, 4 * FS), lambda i, w: (w[1 + block], 0)),
        ]

    half = pl.BlockSpec((FS, TILE), lambda i, w: (0, w[0] * PER_HALF + i))
    outs = pl.pallas_call(
        kernel,
        grid_spec=pltpu.PrefetchScalarGridSpec(
            num_scalar_prefetch=1,
            grid=(PER_HALF,),
            in_specs=[spec for block in blocks for spec in act_specs(*block)]
            + [half] * 4
            + [pl.BlockSpec(memory_space=pl.ANY)] * len(gates),
            out_specs=[chunk_spec(*c) for c in BACK_CHUNKS for _ in blocks],
            scratch_shapes=[pltpu.VMEM((count * BLOCK, 4 * FS), BF16)],
        ),
        out_shape=[
            jax.ShapeDtypeStruct((BLOCK, width), BF16) for _, width in BACK_CHUNKS for _ in blocks
        ],
        name="back",
        compiler_params=params(mib),
        cost_estimate=cost(
            3 * 2 * count * BLOCK * HALF * 4 * FS,
            3 * 2 * (4 * FS * HALF + count * BLOCK * HALF) + 3 * 12 * count * BLOCK * FS,
        ),
    )(where, *[x for block in blocks for x in (block[1], block[3], factor)], *weights, *gates)
    return [outs[c * count : (c + 1) * count] for c in range(len(BACK_CHUNKS))]


def combine_kernel(collect_ref, hidden_ref, layer_ref, gain_ref, *refs):
    returned = refs[: len(BACK_CHUNKS)]
    moe_ref, attn_ref, scaled_ref = refs[len(BACK_CHUNKS) :]
    collect = collect_ref[...]
    square = jnp.zeros((TOK, 1), F32)
    cross = jnp.zeros((TOK, 1), F32)
    for (low, width), ref in zip(BACK_CHUNKS, returned):
        for half in range(2):
            start = half * HALF + low
            normed = dot(collect, ref[half * TOK : (half + 1) * TOK, :])
            scaled = normed * gain_ref[:, start : start + width]
            stream = hidden_ref[:, start : start + width].astype(F32)
            scaled_ref[:, start : start + width] = scaled
            square = square + jnp.sum(stream * stream, axis=1, keepdims=True)
            cross = cross + jnp.sum(stream * scaled, axis=1, keepdims=True)
    inverse = lax.rsqrt(square / D + 1e-06)
    factor = inverse * inverse * inverse * (cross / D)
    for start in range(0, D, 768):
        cols = slice(start, start + 768)
        moe = inverse * scaled_ref[:, cols] - hidden_ref[:, cols].astype(F32) * factor
        moe_ref[:, cols] = moe.astype(BF16)
        attn_ref[:, cols] = (layer_ref[:, cols].astype(F32) + moe).astype(BF16)


def combine(collect, hidden, layer, gain, returned):
    return pl.pallas_call(
        combine_kernel,
        out_shape=[jax.ShapeDtypeStruct((TOK, D), BF16)] * 2,
        scratch_shapes=[pltpu.VMEM((TOK, D), F32)],
        name="combine",
        compiler_params=params(),
    )(collect, hidden, layer, gain, *returned)


def stack_heads(block):
    return jnp.concatenate(
        [block[:, h * HD : (h + 1) * HD] for h in range(HEADS_STEP)], axis=0
    )


def prob_kernel(where_ref, query_ref, key_ref, value_ref, prob_ref, out_ref):
    key = key_ref[...]
    value_t = value_ref[...].astype(F32).T.astype(BF16)
    key_at = lax.broadcasted_iota(jnp.int32, (LENGTH, HD), 0)
    query_at = lax.broadcasted_iota(jnp.int32, (LENGTH, HD), 1) + where_ref[5] * TOK
    visible = key_at <= query_at
    for h in range(HEADS_STEP):
        cols = slice(h * HD, (h + 1) * HD)
        scores = dot_nt(key, query_ref[:, cols]) * SCALE
        scores = jnp.where(visible, scores, -jnp.inf)
        expo = jnp.exp(scores - jnp.max(scores, axis=0, keepdims=True))
        prob = (expo * (1.0 / jnp.sum(expo, axis=0, keepdims=True))).astype(BF16)
        prob_ref[0, :, cols] = prob
        out_ref[:, cols] = dot(value_t, prob).T


def probs(where, queries, kv):
    steps = STEPS
    return pl.pallas_call(
        prob_kernel,
        grid_spec=pltpu.PrefetchScalarGridSpec(
            num_scalar_prefetch=1,
            grid=(steps,),
            in_specs=[
                pl.BlockSpec((TOK, WIDE), lambda p, w: (0, p)),
                pl.BlockSpec((LENGTH, HD), lambda p, w: (0, p // STEPS_GROUP)),
                pl.BlockSpec((LENGTH, HD), lambda p, w: (0, KV + p // STEPS_GROUP)),
            ],
            out_specs=[
                pl.BlockSpec((1, LENGTH, WIDE), lambda p, w: (p, 0, 0)),
                pl.BlockSpec((TOK, WIDE), lambda p, w: (0, p)),
            ],
        ),
        out_shape=[
            jax.ShapeDtypeStruct((steps, LENGTH, WIDE), BF16),
            jax.ShapeDtypeStruct((TOK, steps * WIDE), F32),
        ],
        name="probs",
        compiler_params=params(60),
        cost_estimate=cost(
            30 * 2 * steps * WIDE * LENGTH * HD * 6,
            30 * 2 * steps * WIDE * LENGTH,
            30 * steps * WIDE * LENGTH,
        ),
    )(where, queries, kv, kv)


def attend_kernel(
    where_ref,
    prob_ref,
    attn_ref,
    query_ref,
    grad_ref,
    value_ref,
    score_ref,
    mine_ref,
    oth_ref,
    dk_ref,
    dv_ref,
):
    step = pl.program_id(1)
    query = stack_heads(query_ref[...])
    grad = stack_heads(grad_ref[...])
    lane = lax.broadcasted_iota(jnp.int32, (WIDE, HD), 1)
    ones = jnp.where(lax.broadcasted_iota(jnp.int32, (LENGTH, HD), 1) < 2, 1.0, 0.0).astype(BF16)
    value_ext = jnp.concatenate([value_ref[...], ones], axis=1)

    delta = jnp.sum(grad.astype(F32) * stack_heads(attn_ref[...]), axis=1, keepdims=True)
    high = delta.astype(BF16).astype(F32)
    extra = jnp.where(lane == 0, -high, jnp.where(lane == 1, high - delta, 0.0))
    grad_ext = jnp.concatenate([grad, extra.astype(BF16)], axis=1)
    prob = prob_ref[0]
    d_score = (prob.astype(F32) * dot_nt(value_ext, grad_ext)).astype(BF16)
    score_ref[0] = d_score
    dk = dot(d_score, query)
    dv = dot(prob, grad)

    @pl.when(step == 0)
    def _():
        dk_ref[...] = dk
        dv_ref[...] = dv

    @pl.when(step > 0)
    def _():
        dk_ref[...] += dk
        dv_ref[...] += dv

    @pl.when(step == STEPS_GROUP - 1)
    def _():
        core = where_ref[0]
        for k, out_k in ((0, 0), (1, 2), (2, 1), (3, 3)):
            z_k = where_ref[1 + k]
            at = pl.multiple_of((2 * z_k + core) * TOK, TOK)
            mine_ref[k, 0] = (dk_ref[pl.ds(at, TOK), :] * SCALE).astype(BF16)
            mine_ref[k, 1] = dv_ref[pl.ds(at, TOK), :].astype(BF16)
            at = pl.multiple_of((2 * z_k + 1 - core) * TOK, TOK)
            oth_ref[out_k, 0] = (dk_ref[pl.ds(at, TOK), :] * SCALE).astype(BF16)
            oth_ref[out_k, 1] = dv_ref[pl.ds(at, TOK), :].astype(BF16)


def attend(where, prob, attn_out, queries, grads, kv):
    at = lambda g, p: g * STEPS_GROUP + p
    heads = pl.BlockSpec((TOK, WIDE), lambda g, p, w: (0, at(g, p)))
    sums = pl.BlockSpec((4, 2, TOK, HD), lambda g, p, w: (0, 0, 0, g))
    sums_shape = jax.ShapeDtypeStruct((4, 2, TOK, KV * HD), BF16)
    return pl.pallas_call(
        attend_kernel,
        grid_spec=pltpu.PrefetchScalarGridSpec(
            num_scalar_prefetch=1,
            grid=(KV, STEPS_GROUP),
            in_specs=[
                pl.BlockSpec((1, LENGTH, WIDE), lambda g, p, w: (at(g, p), 0, 0)),
                heads,
                heads,
                heads,
                pl.BlockSpec((LENGTH, HD), lambda g, p, w: (0, KV + g)),
            ],
            out_specs=[
                pl.BlockSpec((1, LENGTH, WIDE), lambda g, p, w: (at(g, p), 0, 0)),
                sums,
                sums,
            ],
            scratch_shapes=[pltpu.VMEM((LENGTH, HD), F32), pltpu.VMEM((LENGTH, HD), F32)],
        ),
        out_shape=[jax.ShapeDtypeStruct((STEPS, LENGTH, WIDE), BF16), sums_shape, sums_shape],
        name="attend",
        compiler_params=params(60),
        cost_estimate=cost(2 * HEADS * TOK * LENGTH * HD * 6, 4 * HEADS * TOK * LENGTH),
    )(where, prob, attn_out, queries, grads, kv)


def query_kernel(score_ref, key_ref, *refs):
    dq_ref = refs[-1]
    key_t = key_ref[...].astype(F32).T.astype(BF16)
    dq_t = dot(key_t, score_ref[0])
    for h in range(HEADS_STEP):
        cols = slice(h * HD, (h + 1) * HD)
        dq_ref[:, cols] = (dq_t[:, cols].T * SCALE).astype(BF16)


def query_grads(score, kv, low, count, before=None):
    steps = count * STEPS_GROUP
    base = low * STEPS_GROUP
    in_specs = [
        pl.BlockSpec((1, LENGTH, WIDE), lambda p: (base + p, 0, 0)),
        pl.BlockSpec((LENGTH, HD), lambda p: (0, low + p // STEPS_GROUP)),
    ]
    args = [score, kv]
    if before is not None:
        in_specs.append(pl.BlockSpec(memory_space=pl.ANY))
        args.append(before)
    return pl.pallas_call(
        query_kernel,
        grid=(steps,),
        in_specs=in_specs,
        out_specs=pl.BlockSpec((TOK, WIDE), lambda p: (0, base + p)),
        out_shape=jax.ShapeDtypeStruct((TOK, D), BF16),
        input_output_aliases={} if before is None else {2: 0},
        name="query_grads",
        compiler_params=params(60),
        cost_estimate=cost(60 * steps * WIDE * LENGTH * HD, 60 * steps * WIDE * LENGTH),
    )(*args)


def add(*terms):
    total = terms[0].astype(F32)
    for term in terms[1:]:
        total = total + term.astype(F32)
    return total.astype(BF16)


def local(
    hidden_in,
    norm_gain,
    d_layer,
    route_ids,
    route_gates,
    gate_weight,
    up_weight,
    down_weight,
    saved_preact,
    queries,
    key_vectors,
    value_vectors,
):
    pos = lambda z, c: (z % 4) * 2 + c
    ring = [(z, c) for z in range(4) for c in range(2)]
    perm_a = [(pos(z, c), pos(z + 1 - 2 * c, c)) for z, c in ring]
    perm_b = [(pos(z, c), pos(z - 1 + 2 * c, c)) for z, c in ring]
    perm_core = [(pos(z, c), pos(z, 1 - c)) for z, c in ring]
    ring_axes = ("z", "core")
    send_a = lambda x: lax.ppermute(x, ring_axes, perm_a)
    send_b = lambda x: lax.ppermute(x, ring_axes, perm_b)
    send_core = lambda x: lax.ppermute(x, ring_axes, perm_core)
    perm_far = [(pos(z, c), pos(z + 2, c)) for z, c in ring]
    send_far = lambda x: lax.ppermute(x, ring_axes, perm_far)

    def spread(x):
        split = x.reshape(2 * EXPERTS, CAP, x.shape[1])
        return lax.all_to_all(split, ("core", "ep"), 0, 0, tiled=True).reshape(x.shape)

    core = lax.axis_index("core")
    z = lax.axis_index("z")
    toward = 1 - 2 * core
    where = jnp.stack(
        [core, z, (z - toward) % 4, (z + toward) % 4, (z + 2) % 4, 2 * z + core]
    ).astype(jnp.int32)

    layer = d_layer[0]
    saved = jnp.swapaxes(saved_preact[0], 1, 2)
    gate_w, up_w, down_w = gate_weight[0].T, up_weight[0].T, down_weight[0]

    ids, gates = route_ids[0].T, route_gates[0].T
    sent, collect, kv = dispatch(
        ids, gates, layer, key_vectors[0], value_vectors[0], OUT_CHUNKS[0]
    )
    kv = lax.all_gather(kv, ring_axes, axis=0, tiled=True)
    held = [spread(sent)]

    down_oth, gate_oth, up_oth = send_core(down_w), send_core(gate_w), send_core(up_w)
    weights = (gate_w, up_w, gate_oth, up_oth)

    ring_a = [send_a(x) for x in held]
    ring_b = [send_b(x) for x in held]
    ring_c = [send_a(x) for x in ring_a]

    prob, attn_out = probs(where, queries[0], kv)
    near, near_send = act(
        where, [held, ring_a, ring_b], down_w, down_oth, ACT_MIB, (attn_out,)
    )
    factor = factors(where, saved, send_core(saved))
    near_came = send_core(near_send)

    lead = back(
        where, [(2, near, 2, near_came, 1)], factor, weights, LEAD_MIB, (ring_c[0],)
    )
    far, far_send = act(where, [ring_c], down_w, down_oth, 24, (lead[0][0],))
    far_came = send_core(far_send)
    last = back(where, [(3, far, 0, far_came, 0)], factor, weights, 24)
    lead = [[send_a(x) for x in chunk] for chunk in lead]
    rest = back(
        where,
        [(0, near, 0, near_came, 0), (1, near, 1, near_came, 2)],
        factor,
        weights,
        24,
        (last[0][0], lead[0][0]),
    )

    returned = []
    for (direct,), (distant,), (own, merged) in zip(lead, last, rest):
        distant = send_b(distant)
        merged = send_b(add(merged, distant))
        returned.append(spread(add(own, direct, merged)))

    moe, d_attn = combine(collect, hidden_in[0], layer, norm_gain[None, :], returned)
    score, mine, oth = attend(where, prob, attn_out, queries[0], d_attn, kv)
    total = add(mine, send_core(oth))
    d_query = query_grads(score, kv, 0, 2)
    d_query = query_grads(score, kv, 2, 2, d_query)
    d_kv = add(total[0], send_b(total[1]), send_a(total[2]), send_far(total[3]))
    return (moe[None], d_query[None], d_kv[0][None], d_kv[1][None])


def solution(mesh):
    split = Mesh(mesh.devices.reshape(4, 2, 16), ("z", "core", "ep"))
    sp = ("z", "core")
    rows = P("ep", sp, None)
    in_specs = (
        rows,
        P(),
        rows,
        rows,
        rows,
        P("ep", None, sp),
        P("ep", None, sp),
        rows,
        P("ep", None, None, sp),
        rows,
        rows,
        rows,
    )
    return jax.shard_map(
        local, mesh=split, in_specs=in_specs, out_specs=(rows,) * 4, check_vma=False
    )
```

```python
import math

import jax
import jax.numpy as jnp
from jax import lax
from jax.experimental import pallas as pl
from jax.experimental.pallas import tpu as pltpu
from jax.sharding import Mesh, PartitionSpec as P

D = 6144
HALF = 3072
FS = 320
HD = 128
TOK = 128
TOPK = 8
CAP = 8
HEADS = 48
KV = 4
EXPERTS = 16
LENGTH = 1024
BLOCK = 256
GROUP = HEADS // KV
TILE = 768
FACTOR_COST = 2000
PER_HALF = HALF // TILE
HEADS_STEP = 12
WIDE = HEADS_STEP * HD
STEPS = HEADS // HEADS_STEP
STEPS_GROUP = GROUP // HEADS_STEP
OUT_CHUNKS = ((0, 3072),)
BACK_CHUNKS = ((0, 3072),)
SCALE = 1.0 / math.sqrt(HD)
F32 = jnp.float32
BF16 = jnp.bfloat16

NT = (((1,), (1,)), ((), ()))


def params(mib=24):
    return pltpu.CompilerParams(vmem_limit_bytes=mib * 1024 * 1024)


def dot(a, b):
    return jnp.dot(a, b, preferred_element_type=F32)


def dot_nt(a, b):
    return lax.dot_general(a, b, NT, preferred_element_type=F32)


def hold(array, *gates):
    anywhere = pl.BlockSpec(memory_space=pl.ANY)
    return pl.pallas_call(
        lambda *refs: None,
        in_specs=[anywhere] * (1 + len(gates)),
        out_specs=anywhere,
        out_shape=jax.ShapeDtypeStruct(array.shape, array.dtype),
        input_output_aliases={0: 0},
        name="hold",
        compiler_params=params(1),
    )(array, *gates)


def cost(flops, moved, exps=0):
    return pl.CostEstimate(
        flops=int(flops), bytes_accessed=int(moved), transcendentals=int(exps)
    )


def dispatch(ids, gates, rows, key, value, chunk):
    low, width = chunk

    def kernel(ids_ref, gates_ref, rows_ref, key_ref, value_ref, sent_ref, collect_ref, kv_ref):
        kv_ref[:, : KV * HD] = key_ref[...]
        kv_ref[:, KV * HD :] = value_ref[...]
        ids = ids_ref[...]
        gates = gates_ref[...]
        row = lax.broadcasted_iota(jnp.int32, (TOK, TOK), 0)
        col = lax.broadcasted_iota(jnp.int32, (TOK, TOK), 1)
        expert = lax.broadcasted_iota(jnp.int32, (EXPERTS, TOK), 0)
        hit = jnp.zeros((EXPERTS, TOK), F32)
        gate = jnp.zeros((EXPERTS, TOK), F32)
        for k in range(TOPK):
            match = ids[k : k + 1, :] == expert
            hit = hit + jnp.where(match, 1.0, 0.0)
            gate = gate + jnp.where(match, gates[k : k + 1, :], 0.0)
        earlier = jnp.where(row < col, 1.0, 0.0).astype(BF16)
        slot = dot(hit.astype(BF16), earlier)
        want = lax.broadcasted_iota(jnp.int32, (EXPERTS, CAP, TOK), 1).astype(F32)
        pick3 = jnp.where((hit[:, None, :] > 0.5) & (slot[:, None, :] == want), 1.0, 0.0)
        gate3 = jnp.sum(pick3 * gate[:, None, :], axis=2, keepdims=True)
        pick = pick3.reshape(EXPERTS * CAP, TOK)
        gate_col = gate3.reshape(EXPERTS * CAP, 1)
        collect_ref[...] = pick.T.astype(BF16)
        pick = pick.astype(BF16)
        for half in range(2):
            start = half * HALF + low
            picked = dot(pick, rows_ref[:, start : start + width]) * gate_col
            sent_ref[half * TOK : (half + 1) * TOK, :] = picked.astype(BF16)

    whole = lambda x: pl.BlockSpec(x.shape, lambda i: (0,) * x.ndim)
    args = (ids, gates, rows, key, value)
    out_shape = [
        jax.ShapeDtypeStruct((BLOCK, width), BF16),
        jax.ShapeDtypeStruct((TOK, EXPERTS * CAP), BF16),
        jax.ShapeDtypeStruct((TOK, 2 * KV * HD), BF16),
    ]
    return pl.pallas_call(
        kernel,
        grid=(1,),
        in_specs=[whole(x) for x in args],
        out_specs=[whole(x) for x in out_shape],
        out_shape=out_shape,
        name="dispatch",
        compiler_params=params(60),
    )(*args)


def in_chip_order(where_ref, own, oth, axis=0):
    even = where_ref[0] == 0
    return jnp.concatenate([jnp.where(even, own, oth), jnp.where(even, oth, own)], axis=axis)


def factor_kernel(where_ref, saved_ref, saved_oth_ref, _gate_ref, out_ref):
    pieces = []
    for ref in (saved_ref, saved_oth_ref):
        gate = ref[0].astype(F32)
        sg = 1.0 / (1.0 + jnp.exp(-gate))
        pieces.append((ref[1].astype(F32) * sg * (1.0 + gate * (1.0 - sg)), gate * sg))
    for k in range(2):
        both = in_chip_order(where_ref, pieces[0][k], pieces[1][k])
        out_ref[:, k * 2 * FS : (k + 1) * 2 * FS] = both.T.astype(BF16)


def factors(where, saved, saved_oth, gate):
    rows = pl.BlockSpec((2, FS, BLOCK), lambda i, w: (0, 0, i))
    return pl.pallas_call(
        factor_kernel,
        grid_spec=pltpu.PrefetchScalarGridSpec(
            num_scalar_prefetch=1,
            grid=(LENGTH // BLOCK,),
            in_specs=[rows, rows, pl.BlockSpec(memory_space=pl.ANY)],
            out_specs=pl.BlockSpec((BLOCK, 4 * FS), lambda i, w: (i, 0)),
        ),
        out_shape=jax.ShapeDtypeStruct((LENGTH, 4 * FS), BF16),
        name="factors",
        compiler_params=params(16),
        cost_estimate=cost(FACTOR_COST * LENGTH * FS, FACTOR_COST * LENGTH * FS),
    )(where, saved, saved_oth, gate)


def act(where, blocks, down_own, down_oth, mib, scale, gates=()):
    count = len(blocks)
    shape = (count * BLOCK, 2 * FS)

    def kernel(where_ref, *refs):
        part_refs = refs[: count * len(OUT_CHUNKS)]
        own_ref, oth_ref = refs[count * len(OUT_CHUNKS) :][:2]
        total_ref, send_ref = refs[-2:]
        step = pl.program_id(0)
        weight = in_chip_order(where_ref, own_ref[...], oth_ref[...])

        @pl.when(step == 0)
        def _():
            total_ref[...] = jnp.zeros_like(total_ref)

        for c, (low, width) in enumerate(OUT_CHUNKS):
            start = low // TILE

            @pl.when((step >= start) & (step < start + width // TILE))
            def _():
                refs_c = part_refs[c * count : (c + 1) * count]
                rows = jnp.concatenate([ref[...] for ref in refs_c], axis=0)
                total_ref[...] += dot_nt(rows, weight)

        @pl.when(step == pl.num_programs(0) - 1)
        def _():
            send_ref[...] = total_ref[...].astype(BF16)

    whole = pl.BlockSpec(shape, lambda i, w: (0, 0))
    half = pl.BlockSpec((FS, TILE), lambda i, w: (0, w[0] * PER_HALF + i))
    parts = [block[c] for c in range(len(OUT_CHUNKS)) for block in blocks]
    return pl.pallas_call(
        kernel,
        grid_spec=pltpu.PrefetchScalarGridSpec(
            num_scalar_prefetch=1,
            grid=(PER_HALF,),
            in_specs=[chunk_spec(*c) for c in OUT_CHUNKS for _ in blocks]
            + [half, half]
            + [pl.BlockSpec(memory_space=pl.ANY)] * len(gates),
            out_specs=[whole, whole],
        ),
        out_shape=[jax.ShapeDtypeStruct(shape, F32), jax.ShapeDtypeStruct(shape, BF16)],
        name="act",
        compiler_params=params(mib),
        cost_estimate=cost(
            scale * 2 * count * BLOCK * HALF * 2 * FS,
            scale * 2 * (count * BLOCK * HALF + 2 * FS * HALF),
        ),
    )(where, *parts, down_own, down_oth, *gates)


def chunk_spec(low, width):
    start, steps = low // TILE, width // TILE
    return pl.BlockSpec((BLOCK, TILE), lambda i, w: (0, jnp.clip(i - start, 0, steps - 1)))


def back(where, blocks, factor, weights, mib, scale, gates=()):
    count = len(blocks)

    def kernel(where_ref, *refs):
        act_refs, refs = refs[: 3 * count], refs[3 * count :]
        gate_own, up_own, gate_oth, up_oth = refs[:4]
        out_refs, pre_ref = refs[4 + len(gates) : -1], refs[-1]
        step = pl.program_id(0)

        @pl.when(step == 0)
        def _():
            for k in range(count):
                mine_ref, came_ref, factor_ref = act_refs[3 * k : 3 * k + 3]
                d_act = mine_ref[...] + came_ref[...].astype(F32)
                for side in range(2):
                    cols = slice(side * 2 * FS, (side + 1) * 2 * FS)
                    scaled = d_act * factor_ref[:, cols].astype(F32)
                    pre_ref[k * BLOCK : (k + 1) * BLOCK, cols] = scaled.astype(BF16)

        gate = in_chip_order(where_ref, gate_own[...], gate_oth[...])
        up = in_chip_order(where_ref, up_own[...], up_oth[...])
        weight = jnp.concatenate([gate, up], axis=0)
        total = dot(pre_ref[...], weight).astype(BF16)
        for c, (low, width) in enumerate(BACK_CHUNKS):
            start = low // TILE

            @pl.when((step >= start) & (step < start + width // TILE))
            def _():
                for k in range(count):
                    out_refs[c * count + k][...] = total[k * BLOCK : (k + 1) * BLOCK]

    def act_specs(block, _mine, at, _came, came_at):
        return [
            pl.BlockSpec((BLOCK, 2 * FS), lambda i, w: (at, 0)),
            pl.BlockSpec((BLOCK, 2 * FS), lambda i, w: (came_at, 0)),
            pl.BlockSpec((BLOCK, 4 * FS), lambda i, w: (w[1 + block], 0)),
        ]

    half = pl.BlockSpec((FS, TILE), lambda i, w: (0, w[0] * PER_HALF + i))
    outs = pl.pallas_call(
        kernel,
        grid_spec=pltpu.PrefetchScalarGridSpec(
            num_scalar_prefetch=1,
            grid=(PER_HALF,),
            in_specs=[spec for block in blocks for spec in act_specs(*block)]
            + [half] * 4
            + [pl.BlockSpec(memory_space=pl.ANY)] * len(gates),
            out_specs=[chunk_spec(*c) for c in BACK_CHUNKS for _ in blocks],
            scratch_shapes=[pltpu.VMEM((count * BLOCK, 4 * FS), BF16)],
        ),
        out_shape=[
            jax.ShapeDtypeStruct((BLOCK, width), BF16) for _, width in BACK_CHUNKS for _ in blocks
        ],
        name="back",
        compiler_params=params(mib),
        cost_estimate=cost(
            scale * 2 * count * BLOCK * HALF * 4 * FS,
            scale * 2 * (4 * FS * HALF + count * BLOCK * HALF),
        ),
    )(where, *[x for block in blocks for x in (block[1], block[3], factor)], *weights, *gates)
    return [outs[c * count : (c + 1) * count] for c in range(len(BACK_CHUNKS))]


def combine_kernel(collect_ref, hidden_ref, layer_ref, gain_ref, *refs):
    returned = refs[: len(BACK_CHUNKS)]
    moe_ref, attn_ref, scaled_ref = refs[len(BACK_CHUNKS) :]
    collect = collect_ref[...]
    square = jnp.zeros((TOK, 1), F32)
    cross = jnp.zeros((TOK, 1), F32)
    for (low, width), ref in zip(BACK_CHUNKS, returned):
        for half in range(2):
            start = half * HALF + low
            normed = dot(collect, ref[half * TOK : (half + 1) * TOK, :])
            scaled = normed * gain_ref[:, start : start + width]
            stream = hidden_ref[:, start : start + width].astype(F32)
            scaled_ref[:, start : start + width] = scaled
            square = square + jnp.sum(stream * stream, axis=1, keepdims=True)
            cross = cross + jnp.sum(stream * scaled, axis=1, keepdims=True)
    inverse = lax.rsqrt(square / D + 1e-06)
    factor = inverse * inverse * inverse * (cross / D)
    for start in range(0, D, 768):
        cols = slice(start, start + 768)
        moe = inverse * scaled_ref[:, cols] - hidden_ref[:, cols].astype(F32) * factor
        moe_ref[:, cols] = moe.astype(BF16)
        attn_ref[:, cols] = (layer_ref[:, cols].astype(F32) + moe).astype(BF16)


def combine(collect, hidden, layer, gain, returned):
    return pl.pallas_call(
        combine_kernel,
        out_shape=[jax.ShapeDtypeStruct((TOK, D), BF16)] * 2,
        scratch_shapes=[pltpu.VMEM((TOK, D), F32)],
        name="combine",
        compiler_params=params(),
    )(collect, hidden, layer, gain, *returned)


def stack_heads(block):
    return jnp.concatenate(
        [block[:, h * HD : (h + 1) * HD] for h in range(HEADS_STEP)], axis=0
    )


def prob_kernel(
    where_ref,
    query_ref,
    key_ref,
    value_ref,
    held_ref,
    own_ref,
    oth_ref,
    prob_ref,
    out_ref,
    home_ref,
    send_ref,
):
    step = pl.program_id(0)

    @pl.when(step < PER_HALF)
    def _():
        weight = in_chip_order(where_ref, own_ref[...], oth_ref[...])
        term = dot_nt(held_ref[...], weight)
        total = jnp.where(step == 0, 0.0, home_ref[...]) + term
        home_ref[...] = total
        send_ref[...] = total.astype(BF16)

    @pl.when(step >= PER_HALF)
    def _():
        key = key_ref[...]
        value_t = value_ref[...].astype(F32).T.astype(BF16)
        key_at = lax.broadcasted_iota(jnp.int32, (LENGTH, HD), 0)
        query_at = lax.broadcasted_iota(jnp.int32, (LENGTH, HD), 1) + where_ref[5] * TOK
        visible = key_at <= query_at
        for h in range(HEADS_STEP):
            cols = slice(h * HD, (h + 1) * HD)
            scores = dot_nt(key, query_ref[:, cols]) * SCALE
            scores = jnp.where(visible, scores, -jnp.inf)
            expo = jnp.exp(scores - jnp.max(scores, axis=0, keepdims=True))
            prob = (expo * (1.0 / jnp.sum(expo, axis=0, keepdims=True))).astype(BF16)
            prob_ref[0, :, cols] = prob
            out_ref[:, cols] = dot(value_t, prob).T


def probs(where, queries, kv, held, down_own, down_oth):
    tile = lambda i: jnp.minimum(i, PER_HALF - 1)
    at = lambda i: jnp.maximum(i - PER_HALF, 0)
    half = pl.BlockSpec((FS, TILE), lambda i, w: (0, w[0] * PER_HALF + tile(i)))
    whole = pl.BlockSpec((BLOCK, 2 * FS), lambda i, w: (0, 0))
    return pl.pallas_call(
        prob_kernel,
        grid_spec=pltpu.PrefetchScalarGridSpec(
            num_scalar_prefetch=1,
            grid=(PER_HALF + STEPS,),
            in_specs=[
                pl.BlockSpec((TOK, WIDE), lambda i, w: (0, at(i))),
                pl.BlockSpec((LENGTH, HD), lambda i, w: (0, at(i) // STEPS_GROUP)),
                pl.BlockSpec((LENGTH, HD), lambda i, w: (0, KV + at(i) // STEPS_GROUP)),
                pl.BlockSpec((BLOCK, TILE), lambda i, w: (0, tile(i))),
                half,
                half,
            ],
            out_specs=[
                pl.BlockSpec((1, LENGTH, WIDE), lambda i, w: (at(i), 0, 0)),
                pl.BlockSpec((TOK, WIDE), lambda i, w: (0, at(i))),
                whole,
                whole,
            ],
        ),
        out_shape=[
            jax.ShapeDtypeStruct((STEPS, LENGTH, WIDE), BF16),
            jax.ShapeDtypeStruct((TOK, D), F32),
            jax.ShapeDtypeStruct((BLOCK, 2 * FS), F32),
            jax.ShapeDtypeStruct((BLOCK, 2 * FS), BF16),
        ],
        name="probs",
        compiler_params=params(32),
        cost_estimate=cost(
            30 * 2 * HEADS * TOK * LENGTH * HD * 6,
            30 * 2 * HEADS * TOK * LENGTH,
            30 * HEADS * TOK * LENGTH,
        ),
    )(where, queries, kv, kv, held, down_own, down_oth)


def attend_kernel(
    where_ref,
    prob_ref,
    attn_ref,
    query_ref,
    grad_ref,
    value_ref,
    score_ref,
    mine_ref,
    oth_ref,
    dk_ref,
    dv_ref,
):
    step = pl.program_id(1)
    query = stack_heads(query_ref[...])
    grad = stack_heads(grad_ref[...])
    lane = lax.broadcasted_iota(jnp.int32, (WIDE, HD), 1)
    ones = jnp.where(lax.broadcasted_iota(jnp.int32, (LENGTH, HD), 1) < 2, 1.0, 0.0).astype(BF16)
    value_ext = jnp.concatenate([value_ref[...], ones], axis=1)

    delta = jnp.sum(grad.astype(F32) * stack_heads(attn_ref[...]), axis=1, keepdims=True)
    high = delta.astype(BF16).astype(F32)
    extra = jnp.where(lane == 0, -high, jnp.where(lane == 1, high - delta, 0.0))
    grad_ext = jnp.concatenate([grad, extra.astype(BF16)], axis=1)
    prob = prob_ref[0]
    d_score = (prob.astype(F32) * dot_nt(value_ext, grad_ext)).astype(BF16)
    score_ref[0] = d_score
    dk = dot(d_score, query)
    dv = dot(prob, grad)

    @pl.when(step == 0)
    def _():
        dk_ref[...] = dk
        dv_ref[...] = dv

    @pl.when(step > 0)
    def _():
        dk_ref[...] += dk
        dv_ref[...] += dv

    @pl.when(step == STEPS_GROUP - 1)
    def _():
        core = where_ref[0]
        for k, out_k in ((0, 0), (1, 2), (2, 1), (3, 3)):
            z_k = where_ref[1 + k]
            at = pl.multiple_of((2 * z_k + core) * TOK, TOK)
            mine_ref[k, 0] = (dk_ref[pl.ds(at, TOK), :] * SCALE).astype(BF16)
            mine_ref[k, 1] = dv_ref[pl.ds(at, TOK), :].astype(BF16)
            at = pl.multiple_of((2 * z_k + 1 - core) * TOK, TOK)
            oth_ref[out_k, 0] = (dk_ref[pl.ds(at, TOK), :] * SCALE).astype(BF16)
            oth_ref[out_k, 1] = dv_ref[pl.ds(at, TOK), :].astype(BF16)


def attend(where, prob, attn_out, queries, grads, kv):
    at = lambda g, p: g * STEPS_GROUP + p
    heads = pl.BlockSpec((TOK, WIDE), lambda g, p, w: (0, at(g, p)))
    sums = pl.BlockSpec((4, 2, TOK, HD), lambda g, p, w: (0, 0, 0, g))
    sums_shape = jax.ShapeDtypeStruct((4, 2, TOK, KV * HD), BF16)
    return pl.pallas_call(
        attend_kernel,
        grid_spec=pltpu.PrefetchScalarGridSpec(
            num_scalar_prefetch=1,
            grid=(KV, STEPS_GROUP),
            in_specs=[
                pl.BlockSpec((1, LENGTH, WIDE), lambda g, p, w: (at(g, p), 0, 0)),
                heads,
                heads,
                heads,
                pl.BlockSpec((LENGTH, HD), lambda g, p, w: (0, KV + g)),
            ],
            out_specs=[
                pl.BlockSpec((1, LENGTH, WIDE), lambda g, p, w: (at(g, p), 0, 0)),
                sums,
                sums,
            ],
            scratch_shapes=[pltpu.VMEM((LENGTH, HD), F32), pltpu.VMEM((LENGTH, HD), F32)],
        ),
        out_shape=[jax.ShapeDtypeStruct((STEPS, LENGTH, WIDE), BF16), sums_shape, sums_shape],
        name="attend",
        compiler_params=params(42),
        cost_estimate=cost(2 * HEADS * TOK * LENGTH * HD * 6, 4 * HEADS * TOK * LENGTH),
    )(where, prob, attn_out, queries, grads, kv)


def query_kernel(score_ref, key_ref, *refs):
    dq_ref = refs[-1]
    key_t = key_ref[...].astype(F32).T.astype(BF16)
    dq_t = dot(key_t, score_ref[0])
    for h in range(HEADS_STEP):
        cols = slice(h * HD, (h + 1) * HD)
        dq_ref[:, cols] = (dq_t[:, cols].T * SCALE).astype(BF16)


def query_grads(score, kv, low, count, before=None):
    steps = count * STEPS_GROUP
    base = low * STEPS_GROUP
    in_specs = [
        pl.BlockSpec((1, LENGTH, WIDE), lambda p: (base + p, 0, 0)),
        pl.BlockSpec((LENGTH, HD), lambda p: (0, low + p // STEPS_GROUP)),
    ]
    args = [score, kv]
    if before is not None:
        in_specs.append(pl.BlockSpec(memory_space=pl.ANY))
        args.append(before)
    return pl.pallas_call(
        query_kernel,
        grid=(steps,),
        in_specs=in_specs,
        out_specs=pl.BlockSpec((TOK, WIDE), lambda p: (0, base + p)),
        out_shape=jax.ShapeDtypeStruct((TOK, D), BF16),
        input_output_aliases={} if before is None else {2: 0},
        name="query_grads",
        compiler_params=params(60),
        cost_estimate=cost(60 * steps * WIDE * LENGTH * HD, 60 * steps * WIDE * LENGTH),
    )(*args)


def add(*terms):
    total = terms[0].astype(F32)
    for term in terms[1:]:
        total = total + term.astype(F32)
    return total.astype(BF16)


def local(
    hidden_in,
    norm_gain,
    d_layer,
    route_ids,
    route_gates,
    gate_weight,
    up_weight,
    down_weight,
    saved_preact,
    queries,
    key_vectors,
    value_vectors,
):
    pos = lambda z, c: (z % 4) * 2 + c
    ring = [(z, c) for z in range(4) for c in range(2)]
    perm_a = [(pos(z, c), pos(z + 1 - 2 * c, c)) for z, c in ring]
    perm_b = [(pos(z, c), pos(z - 1 + 2 * c, c)) for z, c in ring]
    perm_core = [(pos(z, c), pos(z, 1 - c)) for z, c in ring]
    ring_axes = ("z", "core")
    send_a = lambda x: lax.ppermute(x, ring_axes, perm_a)
    send_b = lambda x: lax.ppermute(x, ring_axes, perm_b)
    send_core = lambda x: lax.ppermute(x, ring_axes, perm_core)
    perm_far = [(pos(z, c), pos(z + 2, c)) for z, c in ring]
    send_far = lambda x: lax.ppermute(x, ring_axes, perm_far)

    def spread(x):
        split = x.reshape(2 * EXPERTS, CAP, x.shape[1])
        return lax.all_to_all(split, ("core", "ep"), 0, 0, tiled=True).reshape(x.shape)

    core = lax.axis_index("core")
    z = lax.axis_index("z")
    toward = 1 - 2 * core
    where = jnp.stack(
        [core, z, (z - toward) % 4, (z + toward) % 4, (z + 2) % 4, 2 * z + core]
    ).astype(jnp.int32)

    layer = d_layer[0]
    saved = jnp.swapaxes(saved_preact[0], 1, 2)
    gate_w, up_w, down_w = gate_weight[0].T, up_weight[0].T, down_weight[0]

    ids, gates = route_ids[0].T, route_gates[0].T
    sent, collect, kv = dispatch(
        ids, gates, layer, key_vectors[0], value_vectors[0], OUT_CHUNKS[0]
    )
    kv = lax.all_gather(kv, ring_axes, axis=0, tiled=True)
    held = [spread(sent)]

    down_oth, gate_oth, up_oth = send_core(down_w), send_core(gate_w), send_core(up_w)
    weights = (gate_w, up_w, gate_oth, up_oth)

    prob, attn_out, home, home_send = probs(
        where, queries[0], kv, held[0], down_w, down_oth
    )
    factor = factors(where, saved, send_core(saved), attn_out)
    ring_a = [hold(send_a(x), factor) for x in held]
    ring_b = [send_b(x) for x in held]
    ring_c = [send_a(x) for x in ring_a]
    near, near_send = act(where, [ring_a, ring_b], down_w, down_oth, 24, 30, (factor,))
    near_came = send_core(near_send)
    home_came = send_core(home_send)

    lead = back(
        where, [(2, near, 1, near_came, 0)], factor, weights, 24, 0.01, ()
    )
    far, far_send = act(where, [ring_c], down_w, down_oth, 24, 3, (lead[0][0],))
    far_came = send_core(far_send)
    last = back(where, [(3, far, 0, far_came, 0)], factor, weights, 24, 3)
    lead = [[send_a(x) for x in chunk] for chunk in lead]
    rest = back(
        where,
        [(0, home, 0, home_came, 0), (1, near, 0, near_came, 1)],
        factor,
        weights,
        24,
        3,
        (last[0][0], lead[0][0]),
    )

    returned = []
    for (direct,), (distant,), (own, merged) in zip(lead, last, rest):
        distant = send_b(distant)
        merged = send_b(add(merged, distant))
        returned.append(spread(add(own, direct, merged)))

    moe, d_attn = combine(collect, hidden_in[0], layer, norm_gain[None, :], returned)
    score, mine, oth = attend(where, prob, attn_out, queries[0], d_attn, kv)
    total = add(mine, send_core(oth))
    d_query = query_grads(score, kv, 0, 1)
    d_query = query_grads(score, kv, 1, 3, d_query)
    d_kv = add(total[0], send_b(total[1]), send_a(total[2]), send_far(total[3]))
    return (moe[None], d_query[None], d_kv[0][None], d_kv[1][None])


def solution(mesh):
    split = Mesh(mesh.devices.reshape(4, 2, 16), ("z", "core", "ep"))
    sp = ("z", "core")
    rows = P("ep", sp, None)
    in_specs = (
        rows,
        P(),
        rows,
        rows,
        rows,
        P("ep", None, sp),
        P("ep", None, sp),
        rows,
        P("ep", None, None, sp),
        rows,
        rows,
        rows,
    )
    return jax.shard_map(
        local, mesh=split, in_specs=in_specs, out_specs=(rows,) * 4, check_vma=False
    )
```

```python
import math

import jax
import jax.numpy as jnp
from jax import lax
from jax.experimental import pallas as pl
from jax.experimental.pallas import tpu as pltpu
from jax.sharding import Mesh, PartitionSpec as P

D = 6144
HALF = 3072
FS = 320
HD = 128
TOK = 128
TOPK = 8
CAP = 8
HEADS = 48
KV = 4
EXPERTS = 16
LENGTH = 1024
BLOCK = 256
GROUP = HEADS // KV
TILE = 1536
FACTOR_COST = 2000
PER_HALF = HALF // TILE
HEADS_STEP = 12
WIDE = HEADS_STEP * HD
STEPS = HEADS // HEADS_STEP
STEPS_GROUP = GROUP // HEADS_STEP
OUT_CHUNKS = ((0, 3072),)
BACK_CHUNKS = ((0, 3072),)
SCALE = 1.0 / math.sqrt(HD)
F32 = jnp.float32
BF16 = jnp.bfloat16

NT = (((1,), (1,)), ((), ()))


def params(mib=24):
    return pltpu.CompilerParams(vmem_limit_bytes=mib * 1024 * 1024)


def dot(a, b):
    return jnp.dot(a, b, preferred_element_type=F32)


def dot_nt(a, b):
    return lax.dot_general(a, b, NT, preferred_element_type=F32)


def hold(array, *gates):
    anywhere = pl.BlockSpec(memory_space=pl.ANY)
    return pl.pallas_call(
        lambda *refs: None,
        in_specs=[anywhere] * (1 + len(gates)),
        out_specs=anywhere,
        out_shape=jax.ShapeDtypeStruct(array.shape, array.dtype),
        input_output_aliases={0: 0},
        name="hold",
        compiler_params=params(1),
    )(array, *gates)


def cost(flops, moved, exps=0):
    return pl.CostEstimate(
        flops=int(flops), bytes_accessed=int(moved), transcendentals=int(exps)
    )


def dispatch(ids, gates, rows, key, value, chunk):
    low, width = chunk

    def kernel(ids_ref, gates_ref, rows_ref, key_ref, value_ref, sent_ref, collect_ref, kv_ref):
        kv_ref[:, : KV * HD] = key_ref[...]
        kv_ref[:, KV * HD :] = value_ref[...]
        ids = ids_ref[...]
        gates = gates_ref[...]
        row = lax.broadcasted_iota(jnp.int32, (TOK, TOK), 0)
        col = lax.broadcasted_iota(jnp.int32, (TOK, TOK), 1)
        expert = lax.broadcasted_iota(jnp.int32, (EXPERTS, TOK), 0)
        hit = jnp.zeros((EXPERTS, TOK), F32)
        gate = jnp.zeros((EXPERTS, TOK), F32)
        for k in range(TOPK):
            match = ids[k : k + 1, :] == expert
            hit = hit + jnp.where(match, 1.0, 0.0)
            gate = gate + jnp.where(match, gates[k : k + 1, :], 0.0)
        earlier = jnp.where(row < col, 1.0, 0.0).astype(BF16)
        slot = dot(hit.astype(BF16), earlier)
        want = lax.broadcasted_iota(jnp.int32, (EXPERTS, CAP, TOK), 1).astype(F32)
        pick3 = jnp.where((hit[:, None, :] > 0.5) & (slot[:, None, :] == want), 1.0, 0.0)
        gate3 = jnp.sum(pick3 * gate[:, None, :], axis=2, keepdims=True)
        pick = pick3.reshape(EXPERTS * CAP, TOK)
        gate_col = gate3.reshape(EXPERTS * CAP, 1)
        collect_ref[...] = pick.T.astype(BF16)
        pick = pick.astype(BF16)
        for half in range(2):
            start = half * HALF + low
            picked = dot(pick, rows_ref[:, start : start + width]) * gate_col
            sent_ref[half * TOK : (half + 1) * TOK, :] = picked.astype(BF16)

    whole = lambda x: pl.BlockSpec(x.shape, lambda i: (0,) * x.ndim)
    args = (ids, gates, rows, key, value)
    out_shape = [
        jax.ShapeDtypeStruct((BLOCK, width), BF16),
        jax.ShapeDtypeStruct((TOK, EXPERTS * CAP), BF16),
        jax.ShapeDtypeStruct((TOK, 2 * KV * HD), BF16),
    ]
    return pl.pallas_call(
        kernel,
        grid=(1,),
        in_specs=[whole(x) for x in args],
        out_specs=[whole(x) for x in out_shape],
        out_shape=out_shape,
        name="dispatch",
        compiler_params=params(60),
    )(*args)


def in_chip_order(where_ref, own, oth, axis=0):
    even = where_ref[0] == 0
    return jnp.concatenate([jnp.where(even, own, oth), jnp.where(even, oth, own)], axis=axis)


def factor_kernel(where_ref, saved_ref, saved_oth_ref, _gate_ref, out_ref):
    pieces = []
    for ref in (saved_ref, saved_oth_ref):
        gate = ref[0].astype(F32)
        sg = 1.0 / (1.0 + jnp.exp(-gate))
        pieces.append((ref[1].astype(F32) * sg * (1.0 + gate * (1.0 - sg)), gate * sg))
    for k in range(2):
        both = in_chip_order(where_ref, pieces[0][k], pieces[1][k])
        out_ref[:, k * 2 * FS : (k + 1) * 2 * FS] = both.T.astype(BF16)


def factors(where, saved, saved_oth, gate):
    rows = pl.BlockSpec((2, FS, BLOCK), lambda i, w: (0, 0, i))
    return pl.pallas_call(
        factor_kernel,
        grid_spec=pltpu.PrefetchScalarGridSpec(
            num_scalar_prefetch=1,
            grid=(LENGTH // BLOCK,),
            in_specs=[rows, rows, pl.BlockSpec(memory_space=pl.ANY)],
            out_specs=pl.BlockSpec((BLOCK, 4 * FS), lambda i, w: (i, 0)),
        ),
        out_shape=jax.ShapeDtypeStruct((LENGTH, 4 * FS), BF16),
        name="factors",
        compiler_params=params(16),
        cost_estimate=cost(FACTOR_COST * LENGTH * FS, FACTOR_COST * LENGTH * FS),
    )(where, saved, saved_oth, gate)


def act(where, blocks, down_own, down_oth, mib, scale, gates=()):
    count = len(blocks)
    shape = (count * BLOCK, 2 * FS)

    def kernel(where_ref, *refs):
        part_refs = refs[: count * len(OUT_CHUNKS)]
        own_ref, oth_ref = refs[count * len(OUT_CHUNKS) :][:2]
        total_ref, send_ref = refs[-2:]
        step = pl.program_id(0)
        weight = in_chip_order(where_ref, own_ref[...], oth_ref[...])

        @pl.when(step == 0)
        def _():
            total_ref[...] = jnp.zeros_like(total_ref)

        for c, (low, width) in enumerate(OUT_CHUNKS):
            start = low // TILE

            @pl.when((step >= start) & (step < start + width // TILE))
            def _():
                refs_c = part_refs[c * count : (c + 1) * count]
                rows = jnp.concatenate([ref[...] for ref in refs_c], axis=0)
                total_ref[...] += dot_nt(rows, weight)

        @pl.when(step == pl.num_programs(0) - 1)
        def _():
            send_ref[...] = total_ref[...].astype(BF16)

    whole = pl.BlockSpec(shape, lambda i, w: (0, 0))
    half = pl.BlockSpec((FS, TILE), lambda i, w: (0, w[0] * PER_HALF + i))
    parts = [block[c] for c in range(len(OUT_CHUNKS)) for block in blocks]
    return pl.pallas_call(
        kernel,
        grid_spec=pltpu.PrefetchScalarGridSpec(
            num_scalar_prefetch=1,
            grid=(PER_HALF,),
            in_specs=[chunk_spec(*c) for c in OUT_CHUNKS for _ in blocks]
            + [half, half]
            + [pl.BlockSpec(memory_space=pl.ANY)] * len(gates),
            out_specs=[whole, whole],
        ),
        out_shape=[jax.ShapeDtypeStruct(shape, F32), jax.ShapeDtypeStruct(shape, BF16)],
        name="act",
        compiler_params=params(mib),
        cost_estimate=cost(
            scale * 2 * count * BLOCK * HALF * 2 * FS,
            scale * 2 * (count * BLOCK * HALF + 2 * FS * HALF),
        ),
    )(where, *parts, down_own, down_oth, *gates)


def chunk_spec(low, width):
    start, steps = low // TILE, width // TILE
    return pl.BlockSpec((BLOCK, TILE), lambda i, w: (0, jnp.clip(i - start, 0, steps - 1)))


def back(where, blocks, factor, weights, mib, scale, gates=()):
    count = len(blocks)

    def kernel(where_ref, *refs):
        act_refs, refs = refs[: 3 * count], refs[3 * count :]
        gate_own, up_own, gate_oth, up_oth = refs[:4]
        out_refs, pre_ref = refs[4 + len(gates) : -1], refs[-1]
        step = pl.program_id(0)

        @pl.when(step == 0)
        def _():
            for k in range(count):
                mine_ref, came_ref, factor_ref = act_refs[3 * k : 3 * k + 3]
                d_act = mine_ref[...] + came_ref[...].astype(F32)
                for side in range(2):
                    cols = slice(side * 2 * FS, (side + 1) * 2 * FS)
                    scaled = d_act * factor_ref[:, cols].astype(F32)
                    pre_ref[k * BLOCK : (k + 1) * BLOCK, cols] = scaled.astype(BF16)

        gate = in_chip_order(where_ref, gate_own[...], gate_oth[...])
        up = in_chip_order(where_ref, up_own[...], up_oth[...])
        weight = jnp.concatenate([gate, up], axis=0)
        total = dot(pre_ref[...], weight).astype(BF16)
        for c, (low, width) in enumerate(BACK_CHUNKS):
            start = low // TILE

            @pl.when((step >= start) & (step < start + width // TILE))
            def _():
                for k in range(count):
                    out_refs[c * count + k][...] = total[k * BLOCK : (k + 1) * BLOCK]

    def act_specs(block, _mine, at, _came, came_at):
        return [
            pl.BlockSpec((BLOCK, 2 * FS), lambda i, w: (at, 0)),
            pl.BlockSpec((BLOCK, 2 * FS), lambda i, w: (came_at, 0)),
            pl.BlockSpec((BLOCK, 4 * FS), lambda i, w: (w[1 + block], 0)),
        ]

    half = pl.BlockSpec((FS, TILE), lambda i, w: (0, w[0] * PER_HALF + i))
    outs = pl.pallas_call(
        kernel,
        grid_spec=pltpu.PrefetchScalarGridSpec(
            num_scalar_prefetch=1,
            grid=(PER_HALF,),
            in_specs=[spec for block in blocks for spec in act_specs(*block)]
            + [half] * 4
            + [pl.BlockSpec(memory_space=pl.ANY)] * len(gates),
            out_specs=[chunk_spec(*c) for c in BACK_CHUNKS for _ in blocks],
            scratch_shapes=[pltpu.VMEM((count * BLOCK, 4 * FS), BF16)],
        ),
        out_shape=[
            jax.ShapeDtypeStruct((BLOCK, width), BF16) for _, width in BACK_CHUNKS for _ in blocks
        ],
        name="back",
        compiler_params=params(mib),
        cost_estimate=cost(
            scale * 2 * count * BLOCK * HALF * 4 * FS,
            scale * 2 * (4 * FS * HALF + count * BLOCK * HALF),
        ),
    )(where, *[x for block in blocks for x in (block[1], block[3], factor)], *weights, *gates)
    return [outs[c * count : (c + 1) * count] for c in range(len(BACK_CHUNKS))]


def combine_kernel(collect_ref, hidden_ref, layer_ref, gain_ref, *refs):
    returned = refs[: len(BACK_CHUNKS)]
    moe_ref, attn_ref, scaled_ref = refs[len(BACK_CHUNKS) :]
    collect = collect_ref[...]
    square = jnp.zeros((TOK, 1), F32)
    cross = jnp.zeros((TOK, 1), F32)
    for (low, width), ref in zip(BACK_CHUNKS, returned):
        for half in range(2):
            start = half * HALF + low
            normed = dot(collect, ref[half * TOK : (half + 1) * TOK, :])
            scaled = normed * gain_ref[:, start : start + width]
            stream = hidden_ref[:, start : start + width].astype(F32)
            scaled_ref[:, start : start + width] = scaled
            square = square + jnp.sum(stream * stream, axis=1, keepdims=True)
            cross = cross + jnp.sum(stream * scaled, axis=1, keepdims=True)
    inverse = lax.rsqrt(square / D + 1e-06)
    factor = inverse * inverse * inverse * (cross / D)
    for start in range(0, D, 768):
        cols = slice(start, start + 768)
        moe = inverse * scaled_ref[:, cols] - hidden_ref[:, cols].astype(F32) * factor
        moe_ref[:, cols] = moe.astype(BF16)
        attn_ref[:, cols] = (layer_ref[:, cols].astype(F32) + moe).astype(BF16)


def combine(collect, hidden, layer, gain, returned):
    return pl.pallas_call(
        combine_kernel,
        out_shape=[jax.ShapeDtypeStruct((TOK, D), BF16)] * 2,
        scratch_shapes=[pltpu.VMEM((TOK, D), F32)],
        name="combine",
        compiler_params=params(),
    )(collect, hidden, layer, gain, *returned)


def stack_heads(block):
    return jnp.concatenate(
        [block[:, h * HD : (h + 1) * HD] for h in range(HEADS_STEP)], axis=0
    )


def prob_kernel(
    where_ref,
    query_ref,
    key_ref,
    value_ref,
    held_ref,
    own_ref,
    oth_ref,
    prob_ref,
    out_ref,
    home_ref,
    send_ref,
):
    step = pl.program_id(0)

    @pl.when(step < PER_HALF)
    def _():
        weight = in_chip_order(where_ref, own_ref[...], oth_ref[...])
        term = dot_nt(held_ref[...], weight)
        total = jnp.where(step == 0, 0.0, home_ref[...]) + term
        home_ref[...] = total
        send_ref[...] = total.astype(BF16)

    @pl.when(step >= PER_HALF)
    def _():
        key = key_ref[...]
        value_t = value_ref[...].astype(F32).T.astype(BF16)
        key_at = lax.broadcasted_iota(jnp.int32, (LENGTH, HD), 0)
        query_at = lax.broadcasted_iota(jnp.int32, (LENGTH, HD), 1) + where_ref[5] * TOK
        visible = key_at <= query_at
        for h in range(HEADS_STEP):
            cols = slice(h * HD, (h + 1) * HD)
            scores = dot_nt(key, query_ref[:, cols]) * SCALE
            scores = jnp.where(visible, scores, -jnp.inf)
            expo = jnp.exp(scores - jnp.max(scores, axis=0, keepdims=True))
            prob = (expo * (1.0 / jnp.sum(expo, axis=0, keepdims=True))).astype(BF16)
            prob_ref[0, :, cols] = prob
            out_ref[:, cols] = dot(value_t, prob).T


def probs(where, queries, kv, held, down_own, down_oth):
    tile = lambda i: jnp.minimum(i, PER_HALF - 1)
    at = lambda i: jnp.maximum(i - PER_HALF, 0)
    half = pl.BlockSpec((FS, TILE), lambda i, w: (0, w[0] * PER_HALF + tile(i)))
    whole = pl.BlockSpec((BLOCK, 2 * FS), lambda i, w: (0, 0))
    return pl.pallas_call(
        prob_kernel,
        grid_spec=pltpu.PrefetchScalarGridSpec(
            num_scalar_prefetch=1,
            grid=(PER_HALF + STEPS,),
            in_specs=[
                pl.BlockSpec((TOK, WIDE), lambda i, w: (0, at(i))),
                pl.BlockSpec((LENGTH, HD), lambda i, w: (0, at(i) // STEPS_GROUP)),
                pl.BlockSpec((LENGTH, HD), lambda i, w: (0, KV + at(i) // STEPS_GROUP)),
                pl.BlockSpec((BLOCK, TILE), lambda i, w: (0, tile(i))),
                half,
                half,
            ],
            out_specs=[
                pl.BlockSpec((1, LENGTH, WIDE), lambda i, w: (at(i), 0, 0)),
                pl.BlockSpec((TOK, WIDE), lambda i, w: (0, at(i))),
                whole,
                whole,
            ],
        ),
        out_shape=[
            jax.ShapeDtypeStruct((STEPS, LENGTH, WIDE), BF16),
            jax.ShapeDtypeStruct((TOK, D), F32),
            jax.ShapeDtypeStruct((BLOCK, 2 * FS), F32),
            jax.ShapeDtypeStruct((BLOCK, 2 * FS), BF16),
        ],
        name="probs",
        compiler_params=params(32),
        cost_estimate=cost(
            30 * 2 * HEADS * TOK * LENGTH * HD * 6,
            30 * 2 * HEADS * TOK * LENGTH,
            30 * HEADS * TOK * LENGTH,
        ),
    )(where, queries, kv, kv, held, down_own, down_oth)


def attend_kernel(
    where_ref,
    prob_ref,
    attn_ref,
    query_ref,
    grad_ref,
    value_ref,
    score_ref,
    mine_ref,
    oth_ref,
    dk_ref,
    dv_ref,
):
    step = pl.program_id(1)
    query = stack_heads(query_ref[...])
    grad = stack_heads(grad_ref[...])
    lane = lax.broadcasted_iota(jnp.int32, (WIDE, HD), 1)
    ones = jnp.where(lax.broadcasted_iota(jnp.int32, (LENGTH, HD), 1) < 2, 1.0, 0.0).astype(BF16)
    value_ext = jnp.concatenate([value_ref[...], ones], axis=1)

    delta = jnp.sum(grad.astype(F32) * stack_heads(attn_ref[...]), axis=1, keepdims=True)
    high = delta.astype(BF16).astype(F32)
    extra = jnp.where(lane == 0, -high, jnp.where(lane == 1, high - delta, 0.0))
    grad_ext = jnp.concatenate([grad, extra.astype(BF16)], axis=1)
    prob = prob_ref[0]
    d_score = (prob.astype(F32) * dot_nt(value_ext, grad_ext)).astype(BF16)
    score_ref[0] = d_score
    dk = dot(d_score, query)
    dv = dot(prob, grad)

    @pl.when(step == 0)
    def _():
        dk_ref[...] = dk
        dv_ref[...] = dv

    @pl.when(step > 0)
    def _():
        dk_ref[...] += dk
        dv_ref[...] += dv

    @pl.when(step == STEPS_GROUP - 1)
    def _():
        core = where_ref[0]
        for k, out_k in ((0, 0), (1, 2), (2, 1), (3, 3)):
            z_k = where_ref[1 + k]
            at = pl.multiple_of((2 * z_k + core) * TOK, TOK)
            mine_ref[k, 0] = (dk_ref[pl.ds(at, TOK), :] * SCALE).astype(BF16)
            mine_ref[k, 1] = dv_ref[pl.ds(at, TOK), :].astype(BF16)
            at = pl.multiple_of((2 * z_k + 1 - core) * TOK, TOK)
            oth_ref[out_k, 0] = (dk_ref[pl.ds(at, TOK), :] * SCALE).astype(BF16)
            oth_ref[out_k, 1] = dv_ref[pl.ds(at, TOK), :].astype(BF16)


def attend(where, prob, attn_out, queries, grads, kv):
    at = lambda g, p: g * STEPS_GROUP + p
    heads = pl.BlockSpec((TOK, WIDE), lambda g, p, w: (0, at(g, p)))
    sums = pl.BlockSpec((4, 2, TOK, HD), lambda g, p, w: (0, 0, 0, g))
    sums_shape = jax.ShapeDtypeStruct((4, 2, TOK, KV * HD), BF16)
    return pl.pallas_call(
        attend_kernel,
        grid_spec=pltpu.PrefetchScalarGridSpec(
            num_scalar_prefetch=1,
            grid=(KV, STEPS_GROUP),
            in_specs=[
                pl.BlockSpec((1, LENGTH, WIDE), lambda g, p, w: (at(g, p), 0, 0)),
                heads,
                heads,
                heads,
                pl.BlockSpec((LENGTH, HD), lambda g, p, w: (0, KV + g)),
            ],
            out_specs=[
                pl.BlockSpec((1, LENGTH, WIDE), lambda g, p, w: (at(g, p), 0, 0)),
                sums,
                sums,
            ],
            scratch_shapes=[pltpu.VMEM((LENGTH, HD), F32), pltpu.VMEM((LENGTH, HD), F32)],
        ),
        out_shape=[jax.ShapeDtypeStruct((STEPS, LENGTH, WIDE), BF16), sums_shape, sums_shape],
        name="attend",
        compiler_params=params(28),
        cost_estimate=cost(2 * HEADS * TOK * LENGTH * HD * 6, 4 * HEADS * TOK * LENGTH),
    )(where, prob, attn_out, queries, grads, kv)


def query_kernel(score_ref, key_ref, *refs):
    dq_ref = refs[-1]
    key_t = key_ref[...].astype(F32).T.astype(BF16)
    dq_t = dot(key_t, score_ref[0])
    for h in range(HEADS_STEP):
        cols = slice(h * HD, (h + 1) * HD)
        dq_ref[:, cols] = (dq_t[:, cols].T * SCALE).astype(BF16)


def query_grads(score, kv, low, count, before=None):
    steps = count * STEPS_GROUP
    base = low * STEPS_GROUP
    in_specs = [
        pl.BlockSpec((1, LENGTH, WIDE), lambda p: (base + p, 0, 0)),
        pl.BlockSpec((LENGTH, HD), lambda p: (0, low + p // STEPS_GROUP)),
    ]
    args = [score, kv]
    if before is not None:
        in_specs.append(pl.BlockSpec(memory_space=pl.ANY))
        args.append(before)
    return pl.pallas_call(
        query_kernel,
        grid=(steps,),
        in_specs=in_specs,
        out_specs=pl.BlockSpec((TOK, WIDE), lambda p: (0, base + p)),
        out_shape=jax.ShapeDtypeStruct((TOK, D), BF16),
        input_output_aliases={} if before is None else {2: 0},
        name="query_grads",
        compiler_params=params(16),
        cost_estimate=cost(60 * steps * WIDE * LENGTH * HD, 60 * steps * WIDE * LENGTH),
    )(*args)


def add(*terms):
    total = terms[0].astype(F32)
    for term in terms[1:]:
        total = total + term.astype(F32)
    return total.astype(BF16)


def local(
    hidden_in,
    norm_gain,
    d_layer,
    route_ids,
    route_gates,
    gate_weight,
    up_weight,
    down_weight,
    saved_preact,
    queries,
    key_vectors,
    value_vectors,
):
    pos = lambda z, c: (z % 4) * 2 + c
    ring = [(z, c) for z in range(4) for c in range(2)]
    perm_a = [(pos(z, c), pos(z + 1 - 2 * c, c)) for z, c in ring]
    perm_b = [(pos(z, c), pos(z - 1 + 2 * c, c)) for z, c in ring]
    perm_core = [(pos(z, c), pos(z, 1 - c)) for z, c in ring]
    ring_axes = ("z", "core")
    send_a = lambda x: lax.ppermute(x, ring_axes, perm_a)
    send_b = lambda x: lax.ppermute(x, ring_axes, perm_b)
    send_core = lambda x: lax.ppermute(x, ring_axes, perm_core)
    perm_far = [(pos(z, c), pos(z + 2, c)) for z, c in ring]
    send_far = lambda x: lax.ppermute(x, ring_axes, perm_far)

    def spread(x):
        split = x.reshape(2 * EXPERTS, CAP, x.shape[1])
        return lax.all_to_all(split, ("core", "ep"), 0, 0, tiled=True).reshape(x.shape)

    core = lax.axis_index("core")
    z = lax.axis_index("z")
    toward = 1 - 2 * core
    where = jnp.stack(
        [core, z, (z - toward) % 4, (z + toward) % 4, (z + 2) % 4, 2 * z + core]
    ).astype(jnp.int32)

    layer = d_layer[0]
    saved = jnp.swapaxes(saved_preact[0], 1, 2)
    gate_w, up_w, down_w = gate_weight[0].T, up_weight[0].T, down_weight[0]

    ids, gates = route_ids[0].T, route_gates[0].T
    sent, collect, kv = dispatch(
        ids, gates, layer, key_vectors[0], value_vectors[0], OUT_CHUNKS[0]
    )
    kv = lax.all_gather(kv, ring_axes, axis=0, tiled=True)
    held = [spread(sent)]

    down_oth, gate_oth, up_oth = send_core(down_w), send_core(gate_w), send_core(up_w)
    weights = (gate_w, up_w, gate_oth, up_oth)

    prob, attn_out, home, home_send = probs(
        where, queries[0], kv, held[0], down_w, down_oth
    )
    factor = factors(where, saved, send_core(saved), attn_out)
    ring_a = [hold(send_a(x), factor) for x in held]
    ring_b = [send_b(x) for x in held]
    ring_c = [send_a(x) for x in ring_a]
    near, near_send = act(where, [ring_a, ring_b], down_w, down_oth, 24, 30, (factor,))
    near_came = send_core(near_send)
    home_came = send_core(home_send)

    lead = back(
        where, [(2, near, 1, near_came, 0)], factor, weights, 24, 0.01, ()
    )
    far, far_send = act(where, [ring_c], down_w, down_oth, 24, 3, (lead[0][0],))
    far_came = send_core(far_send)
    last = back(where, [(3, far, 0, far_came, 0)], factor, weights, 24, 3)
    lead = [[send_a(x) for x in chunk] for chunk in lead]
    rest = back(
        where,
        [(0, home, 0, home_came, 0), (1, near, 0, near_came, 1)],
        factor,
        weights,
        24,
        3,
        (last[0][0], lead[0][0]),
    )

    returned = []
    for (direct,), (distant,), (own, merged) in zip(lead, last, rest):
        distant = send_b(distant)
        merged = send_b(add(merged, distant))
        returned.append(spread(add(own, direct, merged)))

    moe, d_attn = combine(collect, hidden_in[0], layer, norm_gain[None, :], returned)
    score, mine, oth = attend(where, prob, attn_out, queries[0], d_attn, kv)
    total = add(mine, send_core(oth))
    d_query = query_grads(score, kv, 0, 1)
    d_query = query_grads(score, kv, 1, 3, d_query)
    d_kv = add(total[0], send_b(total[1]), send_a(total[2]), send_far(total[3]))
    return (moe[None], d_query[None], d_kv[0][None], d_kv[1][None])


def solution(mesh):
    split = Mesh(mesh.devices.reshape(4, 2, 16), ("z", "core", "ep"))
    sp = ("z", "core")
    rows = P("ep", sp, None)
    in_specs = (
        rows,
        P(),
        rows,
        rows,
        rows,
        P("ep", None, sp),
        P("ep", None, sp),
        rows,
        P("ep", None, None, sp),
        rows,
        rows,
        rows,
    )
    return jax.shard_map(
        local, mesh=split, in_specs=in_specs, out_specs=(rows,) * 4, check_vma=False
    )
```
